128 devices in a mesh: blk: 32 (over z, y_lo, x), rel: 4 (over y_hi, core).
Axes of the slice: x: 4, y: 4 (y_hi: 2, y_lo: 2; y = y_hi * 2 + y_lo), z: 4, core: 2. Of those that a mesh axis runs over, the one named last changes fastest.
Arguments:
- left: float32 [131072, 400], P(('blk', 'rel')), may hold values from -1.5 to 1.5
- left_state: float32 [131072], P(('blk', 'rel')), may hold values from 0.02 to 1
- right: float32 [131072, 400], P(('blk', 'rel')), may hold values from -1.5 to 1.5
- right_state: float32 [131072], P(('blk', 'rel')), may hold values from 0.02 to 1
- operators: bfloat16 [24, 400, 400], P('rel'), may hold values from -0.3125 to 0.3125
- need_list: int32 [128, 4, 4], P(('blk', 'rel')), may hold values from -1 to 23, as said below
- block_slot: int32 [128, 3, 8], P(('blk', 'rel')), may hold values from 0 to 15, as said below
- sources: int32 [128, 3, 2048], P(('blk', 'rel')), may hold values from 0 to 1023
- targets: int32 [128, 3, 2048], P(('blk', 'rel')), may hold values from 0 to 1023
- negatives: int32 [128, 3, 8, 256], P(('blk', 'rel')), may hold values from 0 to 1023
Outputs:
- new_left: float32 [131072, 400], P(('blk', 'rel'))
- new_left_state: float32 [131072], P(('blk', 'rel'))
- new_right: float32 [131072, 400], P(('blk', 'rel'))
- new_right_state: float32 [131072], P(('blk', 'rel'))
- op_grad: float32 [24, 160000], P('rel', 'blk')
The draws below stay inside these ranges and needn't reach their ends.
Inputs may be any that keep to these rules, and one draw needn't show every extreme that they name: `need_list`: row o of a device's list holds distinct relations of owner o (ids o * 6 to (o + 1) * 6 - 1) first, then -1; every device fills all 4 slots of some owner. `block_slot`: every entry points at a relation of the list, and every relation of a device's list is named by some block of that device.
All inputs are finite; a program needn't handle non-finite values.
Results may differ from the reference program's by a relative error of at most 0.006.
Values may be sent and summed in bfloat16 or wider, within the bound.
A program may use at most 192 MiB of HBM per device.

```python
import math
import jax
import jax.numpy as jnp
from jax import lax

D = 400
E_DEV = 1024
NBLK = 8
NNEG = 256
BUCKETS = 3
REL_OWN = 6
CAP = 4
NREL = 24
ENT = 131072
EDGES = 2048
N_BLK = 32
N_REL = 4
DEVICES = 128


def needed_counts(key):
    first = jax.random.randint(key, (DEVICES, N_REL), 1, CAP + 1)
    full_owner = jax.random.randint(jax.random.fold_in(key, 7), (DEVICES, 1), 0, N_REL)
    return jnp.where(jnp.arange(N_REL)[None, :] == full_owner, CAP, first).astype(jnp.int32)


def draw_need_list(key, part):
    counts = needed_counts(key)
    key = jax.random.fold_in(key, 11)
    scores = jax.random.randint(key, (DEVICES, N_REL, REL_OWN), 0, 2 ** 20) * REL_OWN + jnp.arange(REL_OWN)
    order = jnp.argsort(scores, axis=-1, stable=True)[..., :CAP].astype(jnp.int32)
    ids = order + (jnp.arange(N_REL) * REL_OWN).astype(jnp.int32)[None, :, None]
    live = jnp.arange(CAP)[None, None, :] < counts[:, :, None]
    return jnp.where(live, ids, -1).astype(jnp.int32)


def draw_block_slot(key, part):
    counts = needed_counts(key)
    key = jax.random.fold_in(key, 23)
    slots = N_REL * CAP
    live = (jnp.arange(CAP)[None, None, :] < counts[:, :, None]).reshape(DEVICES, slots).astype(jnp.int32)
    ranked = jnp.argsort((1 - live) * slots + jnp.arange(slots)[None, :], axis=-1, stable=True).astype(jnp.int32)
    total = jnp.sum(live, axis=-1, keepdims=True)
    blocks = BUCKETS * NBLK
    extra = jax.random.randint(key, (DEVICES, blocks), 0, 2 ** 20) % total
    position = jnp.arange(blocks)[None, :]
    pick = jnp.where(position < total, position, extra).astype(jnp.int32)
    chosen = jnp.take_along_axis(ranked, pick, axis=-1)
    mixing = jax.random.randint(jax.random.fold_in(key, 5), (DEVICES, blocks), 0, 2 ** 20) * blocks + position
    order = jnp.argsort(mixing, axis=-1, stable=True).astype(jnp.int32)
    return jnp.take_along_axis(chosen, order, axis=-1).reshape(DEVICES, BUCKETS, NBLK).astype(jnp.int32)


def place_ends(entries, key, low, top_value):
    shape = entries.shape
    spot = [jax.random.randint(jax.random.fold_in(key, axis), (), 0, shape[axis]) for axis in range(len(shape))]
    entries = entries.at[tuple(spot)].set(low)
    longest = shape.index(max(shape))
    spot[longest] = (spot[longest] + 1) % shape[longest]
    return entries.at[tuple(spot)].set(top_value)


def level_of(key, dims, shards, least, high):
    gain = 1.0
    for dim, shards_of in shards:
        heights = jax.random.uniform(jax.random.fold_in(jax.random.fold_in(key, 6), dim), (shards_of,), jnp.float32, least / len(shards), high / len(shards))
        gain = gain * jnp.repeat(jnp.exp(heights), dims[dim] // shards_of).reshape((-1,) + (1,) * (len(dims) - 1 - dim))
    return gain


def scatter_about(stream_key, shape, deviation, limit, shards=(), held_as=jnp.bfloat16):
    array = deviation * jax.random.normal(stream_key, shape, jnp.float32)
    if shards:
        array = array * level_of(stream_key, shape, shards, -0.22, 0.18)
    return jnp.clip(array, -limit, limit).astype(held_as)


def setup_inputs(seed: int = 0) -> dict:
    key_list = jax.random.split(jax.random.key(seed), 11)
    left = scatter_about(key_list[0], (ENT, D), 0.25, 1.5, ((0, 128),), jnp.float32)
    left_state = jnp.clip(jnp.exp(math.log(1.0) - 3.912023 * jax.random.uniform(key_list[1], (ENT,), jnp.float32) ** level_of(key_list[1], (ENT,), ((0, 128),), -0.2, 0.2)), 0.02, 1.0)
    right = scatter_about(key_list[2], (ENT, D), 0.25, 1.5, ((0, 128),), jnp.float32)
    right_state = jnp.clip(jnp.exp(math.log(1.0) - 3.912023 * jax.random.uniform(key_list[3], (ENT,), jnp.float32) ** level_of(key_list[3], (ENT,), ((0, 128),), -0.2, 0.2)), 0.02, 1.0)
    operators = scatter_about(key_list[4], (NREL, D, D), D ** -0.5, 0.3125, ((0, 4),))
    need_list = draw_need_list(jax.random.fold_in(key_list[10], 71), 0)
    block_slot = draw_block_slot(jax.random.fold_in(key_list[10], 71), 0)
    sources = place_ends(jax.random.randint(key_list[7], (DEVICES, BUCKETS, EDGES), 0, E_DEV), jax.random.fold_in(key_list[7], 1), 0, E_DEV - 1).astype(jnp.int32)
    targets = place_ends(jax.random.randint(key_list[8], (DEVICES, BUCKETS, EDGES), 0, E_DEV), jax.random.fold_in(key_list[8], 1), 0, E_DEV - 1).astype(jnp.int32)
    negatives = place_ends(jax.random.randint(key_list[9], (DEVICES, BUCKETS, NBLK, NNEG), 0, E_DEV), jax.random.fold_in(key_list[9], 1), 0, E_DEV - 1).astype(jnp.int32)
    return dict(left=left, left_state=left_state, right=right, right_state=right_state, operators=operators, need_list=need_list, block_slot=block_slot, sources=sources, targets=targets, negatives=negatives)


step_size = 0.3

def rounded(value):
    return lax.optimization_barrier(value.astype(jnp.bfloat16)).astype(jnp.float32)

def bucket_device(left_rows, left_acc, right_rows, right_acc, ops, src, dst, neg):
    nblk = neg.shape[0]
    width = left_rows.shape[1]
    left_half = left_rows.astype(jnp.bfloat16)
    right_half = right_rows.astype(jnp.bfloat16)
    heads = left_half[src].reshape(nblk, -1, width).astype(jnp.float32)
    tails = right_half[dst].reshape(nblk, -1, width).astype(jnp.float32)
    noise = right_half[neg].astype(jnp.float32)
    ops_full = ops.astype(jnp.float32)
    query = jnp.einsum('bed,bdf->bef', heads, ops_full)
    query_half = rounded(query)
    positive = lax.optimization_barrier(jnp.sum(query * tails, axis=-1))
    negative = jnp.einsum('bef,bnf->ben', query_half, noise)
    pull = -jax.nn.sigmoid(-positive)
    push = rounded(jax.nn.sigmoid(negative) / noise.shape[1])
    grad_query = pull[..., None] * tails + jnp.einsum('ben,bnf->bef', push, noise)
    grad_half = rounded(grad_query)
    grad_heads = jnp.einsum('bef,bdf->bed', grad_half, ops_full)
    grad_ops = jnp.einsum('bed,bef->bdf', heads, grad_half)
    grad_tails = pull[..., None] * query
    grad_noise = jnp.einsum('ben,bef->bnf', push, query_half)
    left_grad = jnp.zeros_like(left_rows).at[src].add(grad_heads.reshape(-1, width))
    right_grad = jnp.zeros_like(right_rows).at[dst].add(grad_tails.reshape(-1, width))
    right_grad = right_grad.at[neg.reshape(-1)].add(grad_noise.reshape(-1, width))
    left_acc = left_acc + lax.optimization_barrier(jnp.mean(left_grad * left_grad, axis=-1))
    left_rows = left_rows - step_size * left_grad / jnp.sqrt(left_acc)[:, None]
    right_acc = right_acc + lax.optimization_barrier(jnp.mean(right_grad * right_grad, axis=-1))
    right_rows = right_rows - step_size * right_grad / jnp.sqrt(right_acc)[:, None]
    return (left_rows, left_acc, right_rows, right_acc, grad_ops)

def reference(left, left_state, right, right_state, operators, need_list, block_slot, sources, targets, negatives):
    devices = N_BLK * N_REL
    left_rows = left.reshape(devices, E_DEV, D)
    left_acc = left_state.reshape(devices, E_DEV)
    right_rows = right.reshape(devices, E_DEV, D)
    right_acc = right_state.reshape(devices, E_DEV)
    need_flat = need_list.reshape(devices, N_REL * CAP)
    rel_id = jnp.take_along_axis(need_flat, block_slot.reshape(devices, BUCKETS * NBLK), axis=1)
    rel_id = rel_id.reshape(devices, BUCKETS, NBLK).astype(jnp.int32)
    grads = jnp.zeros((NREL, D, D), jnp.float32)
    for bucket in range(BUCKETS):

        def per_device(total, item):
            lrow, lacc, rrow, racc, ids, src, dst, neg = item
            lrow, lacc, rrow, racc, grad_ops = bucket_device(lrow, lacc, rrow, racc, operators[ids], src, dst, neg)
            return (total.at[ids].add(grad_ops), (lrow, lacc, rrow, racc))
        grads, (left_rows, left_acc, right_rows, right_acc) = lax.scan(per_device, grads, (left_rows, left_acc, right_rows, right_acc, rel_id[:, bucket], sources[:, bucket], targets[:, bucket], negatives[:, bucket]))
        right_rows = jnp.roll(right_rows.reshape(N_BLK, N_REL, E_DEV, D), 1, axis=0).reshape(devices, E_DEV, D)
        right_acc = jnp.roll(right_acc.reshape(N_BLK, N_REL, E_DEV), 1, axis=0).reshape(devices, E_DEV)
    return (left_rows.reshape(ENT, D), left_acc.reshape(ENT), right_rows.reshape(ENT, D), right_acc.reshape(ENT), grads.reshape(NREL, D * D))
```

```python
import functools
import jax
import jax.numpy as jnp
from jax import lax
from jax.experimental import pallas as pl
from jax.experimental.pallas import tpu as pltpu
from jax.sharding import PartitionSpec as P

BUCKETS = 3
STEP = 0.3
NT = (((1,), (1,)), ((), ()))
TN = (((0,), (0,)), ((), ()))
VMEM_LIMIT = 56 * 1024 * 1024


def onehot(index, rows):
    index = index.astype(jnp.int16)
    row = lax.broadcasted_iota(jnp.int16, (rows, index.shape[1]), 0)
    one = jnp.ones((), jnp.bfloat16)
    return jnp.where(row == index, one, jnp.zeros((), jnp.bfloat16))


def dot(a, b, dims=None):
    if dims is None:
        return jnp.dot(a, b, preferred_element_type=jnp.float32)
    return lax.dot_general(a, b, dims, preferred_element_type=jnp.float32)


def query_step(half_ref, src_ref, op_ref, s_ref, q_ref):
    width = half_ref.shape[0]
    hot = onehot(src_ref[0], half_ref.shape[1])
    s = dot(half_ref[...], hot).astype(jnp.bfloat16)
    s_ref[0] = s
    op = op_ref[0][:width, :width]
    q_ref[0] = dot(op, s, TN).astype(jnp.bfloat16)


def first_kernel(rel_ref, left_ref, src_ref, op_ref, s_ref, q_ref, half_ref):
    @pl.when(pl.program_id(0) == 0)
    def _():
        half_ref[...] = left_ref[...].astype(jnp.bfloat16)

    query_step(half_ref, src_ref, op_ref, s_ref, q_ref)


def first_call(rel, left, src, ops, nblk):
    width, rows = left.shape
    edges = src.shape[-1]
    pad = ops.shape[1:]
    part = lambda k, rel: (k, 0, 0)
    return pl.pallas_call(
        first_kernel,
        grid_spec=pltpu.PrefetchScalarGridSpec(
            num_scalar_prefetch=1,
            grid=(nblk,),
            in_specs=[
                pl.BlockSpec((width, rows), lambda k, rel: (0, 0)),
                pl.BlockSpec((1, 1, edges), part),
                pl.BlockSpec((1,) + pad, lambda k, rel: (rel[k], 0, 0)),
            ],
            out_specs=[pl.BlockSpec((1, width, edges), part)] * 2,
            scratch_shapes=[pltpu.VMEM((width, rows), jnp.bfloat16)],
        ),
        out_shape=[jax.ShapeDtypeStruct((nblk, width, edges), jnp.bfloat16)] * 2,
        compiler_params=pltpu.CompilerParams(vmem_limit_bytes=VMEM_LIMIT),
        name="first_queries",
    )(rel, left, src, ops)


def right_kernel(right_ref, acc_ref, q_ref, tgt_ref, neg_ref, p_ref, new_ref, newacc_ref, half_ref, grad_ref):
    k = pl.program_id(0)
    width, rows = right_ref.shape
    edges = q_ref.shape[2]

    @pl.when(k == 0)
    def _():
        half_ref[...] = right_ref[...].astype(jnp.bfloat16).T
        grad_ref[...] = jnp.zeros_like(grad_ref)

    q = q_ref[0]
    score = dot(half_ref[...], q)
    hits = onehot(neg_ref[0], rows)
    count = dot(hits, jnp.ones((hits.shape[1], 128), jnp.bfloat16)) * (1.0 / hits.shape[1])
    count = jnp.concatenate([count] * (edges // 128), axis=1)
    row = lax.broadcasted_iota(jnp.int32, (rows, edges), 0)
    hit = jnp.where(row == tgt_ref[0], 1.0, 0.0)
    sig = 0.5 * jnp.tanh(0.5 * score) + 0.5
    push = (sig * (count + hit) - hit).astype(jnp.bfloat16)
    p_ref[0] = push
    grad_ref[...] += dot(q, push, NT)

    @pl.when(k == pl.num_programs(0) - 1)
    def _():
        grad = grad_ref[...]
        acc = acc_ref[...] + jnp.sum(grad * grad, axis=0, keepdims=True) * (1.0 / width)
        newacc_ref[...] = acc
        new = right_ref[...].astype(jnp.float32) - STEP * grad * lax.rsqrt(acc)
        new_ref[...] = new.astype(jnp.bfloat16)


def right_call(right, acc, q, tgt, neg):
    width, rows = right.shape
    nblk, _, edges = q.shape
    whole = lambda k: (0, 0)
    part = lambda k: (k, 0, 0)
    return pl.pallas_call(
        right_kernel,
        grid=(nblk,),
        in_specs=[
            pl.BlockSpec((width, rows), whole),
            pl.BlockSpec((1, rows), whole),
            pl.BlockSpec((1, width, edges), part),
            pl.BlockSpec((1, 1, edges), part),
            pl.BlockSpec((1, 1, neg.shape[-1]), part),
        ],
        out_specs=[
            pl.BlockSpec((1, rows, edges), part),
            pl.BlockSpec((width, rows), whole),
            pl.BlockSpec((1, rows), whole),
        ],
        out_shape=[
            jax.ShapeDtypeStruct((nblk, rows, edges), jnp.bfloat16),
            jax.ShapeDtypeStruct((width, rows), jnp.bfloat16),
            jax.ShapeDtypeStruct((1, rows), jnp.float32),
        ],
        scratch_shapes=[pltpu.VMEM((rows, width), jnp.bfloat16), pltpu.VMEM((width, rows), jnp.float32)],
        compiler_params=pltpu.CompilerParams(vmem_limit_bytes=VMEM_LIMIT),
        name="right_update",
    )(right, acc, q, tgt, neg)


def left_kernel(nblk, more, rel_ref, left_ref, acc_ref, right_ref, p_ref, src_ref, op_ref, *rest):
    if more:
        g_ref, new_ref, newacc_ref, s_ref, q_ref, rhalf_ref, half_ref, grad_ref = rest
    else:
        g_ref, new_ref, newacc_ref, rhalf_ref, half_ref, grad_ref = rest
    k = pl.program_id(0)
    width, rows = left_ref.shape

    @pl.when(k == 0)
    def _():
        rhalf_ref[...] = right_ref[...].astype(jnp.bfloat16)
        grad_ref[...] = jnp.zeros_like(grad_ref)

    @pl.when(k < nblk)
    def _():
        g = dot(rhalf_ref[...], p_ref[0]).astype(jnp.bfloat16)
        g_ref[0] = g
        back = dot(op_ref[0][:width, :width], g).astype(jnp.bfloat16)
        grad_ref[...] += dot(back, onehot(src_ref[0], rows), NT)

    @pl.when(k == nblk - 1)
    def _():
        grad = grad_ref[...]
        acc = acc_ref[...] + jnp.sum(grad * grad, axis=0, keepdims=True) * (1.0 / width)
        newacc_ref[...] = acc
        new = left_ref[...] - STEP * grad * lax.rsqrt(acc)
        new_ref[...] = new
        half_ref[...] = new.astype(jnp.bfloat16)

    if more:
        @pl.when(k >= nblk)
        def _():
            query_step(half_ref, src_ref, op_ref, s_ref, q_ref)


def left_call(rel, left, acc, right, p, src, ops, more):
    width, rows = left.shape
    nblk, _, edges = p.shape
    steps = 2 * nblk if more else nblk
    pad = ops.shape[1:]
    whole = lambda k, rel: (0, 0)
    early = lambda k, rel: (jnp.minimum(k, nblk - 1), 0, 0)
    late = lambda k, rel: (jnp.maximum(k - nblk, 0), 0, 0)
    out_specs = [
        pl.BlockSpec((1, width, edges), early),
        pl.BlockSpec((width, rows), whole),
        pl.BlockSpec((1, rows), whole),
    ]
    out_shape = [
        jax.ShapeDtypeStruct((nblk, width, edges), jnp.bfloat16),
        jax.ShapeDtypeStruct((width, rows), jnp.float32),
        jax.ShapeDtypeStruct((1, rows), jnp.float32),
    ]
    if more:
        out_specs += [pl.BlockSpec((1, width, edges), late)] * 2
        out_shape += [jax.ShapeDtypeStruct((nblk, width, edges), jnp.bfloat16)] * 2
    return pl.pallas_call(
        functools.partial(left_kernel, nblk, more),
        grid_spec=pltpu.PrefetchScalarGridSpec(
            num_scalar_prefetch=1,
            grid=(steps,),
            in_specs=[
                pl.BlockSpec((width, rows), whole),
                pl.BlockSpec((1, rows), whole),
                pl.BlockSpec((width, rows), whole),
                pl.BlockSpec((1, rows, edges), early),
                pl.BlockSpec((1, 1, edges), lambda k, rel: (k, 0, 0)),
                pl.BlockSpec((1,) + pad, lambda k, rel: (rel[k], 0, 0)),
            ],
            out_specs=out_specs,
            scratch_shapes=[
                pltpu.VMEM((width, rows), jnp.bfloat16),
                pltpu.VMEM((width, rows), jnp.bfloat16),
                pltpu.VMEM((width, rows), jnp.float32),
            ],
        ),
        out_shape=out_shape,
        compiler_params=pltpu.CompilerParams(vmem_limit_bytes=VMEM_LIMIT),
        cost_estimate=pl.CostEstimate(flops=2 * steps * 320_000_000, bytes_accessed=16_000_000, transcendentals=0),
        name="left_update",
    )(rel, left, acc, right, p, src, ops)


def opgrad_kernel(rel_ref, *refs):
    s_refs, g_refs, out_ref, acc_ref, count_ref, list_ref = refs[:3], refs[3:6], refs[6], refs[7], refs[8], refs[9]
    j = pl.program_id(0)
    nblk = s_refs[0].shape[0]
    width = s_refs[0].shape[1]
    acc_ref[...] = jnp.zeros_like(acc_ref)
    for t in range(3):
        def add(k, carry):
            @pl.when(rel_ref[t * nblk + k] == j)
            def _():
                acc_ref[...] += dot(s_refs[t][k], g_refs[t][k], NT)
            return carry
        lax.fori_loop(0, nblk, add, 0)
    out_ref[0, 0, 0, :, :width] = acc_ref[...].astype(jnp.bfloat16)
    out_ref[0, 0, 0, :, width:] = jnp.zeros((width, out_ref.shape[-1] - width), jnp.bfloat16)


def opgrad_call(rel, s, g, nrel):
    nblk, width, edges = s[0].shape
    whole = pl.BlockSpec((nblk, width, edges), lambda j, rel: (0, 0, 0))

    def place(j, rel):
        owner, i = j // 6, j % 6
        return (owner % 2, i // 2, (owner // 2) * 2 + i % 2, 0, 0)

    return pl.pallas_call(
        opgrad_kernel,
        grid_spec=pltpu.PrefetchScalarGridSpec(
            num_scalar_prefetch=1,
            grid=(nrel,),
            in_specs=[whole] * 6,
            out_specs=pl.BlockSpec((1, 1, 1, width, 512), place),
            scratch_shapes=[pltpu.VMEM((width, width), jnp.float32), pltpu.SMEM((nrel,), jnp.int32), pltpu.SMEM((nrel, 24), jnp.int32)],
        ),
        out_shape=jax.ShapeDtypeStruct((2, 3, 4, width, 512), jnp.bfloat16),
        compiler_params=pltpu.CompilerParams(vmem_limit_bytes=VMEM_LIMIT),
        name="operator_gradients",
    )(rel, *s, *g)
MESH = pl.DeviceIdType.MESH
UNITS = 4
UNIT_ROWS = 112
LANES = 512


def place():
    b, r = lax.axis_index("blk"), lax.axis_index("rel")
    return b // 8, (b // 4) % 2, b % 4, r // 2, r % 2


def device(z, ylo, x, yhi, core):
    return (z * 8 + ylo * 4 + x, yhi * 2 + core)


def greet(peers):
    barrier = pltpu.get_barrier_semaphore()
    for peer in peers:
        pl.semaphore_signal(barrier, inc=1, device_id=peer, device_id_type=MESH)
    pl.semaphore_wait(barrier, len(peers))


def send(src, dst, sems, index, peer):
    copy = pltpu.make_async_remote_copy(
        src_ref=src,
        dst_ref=dst,
        send_sem=sems[0].at[index],
        recv_sem=sems[1].at[index],
        device_id=peer,
        device_id_type=MESH,
    )
    copy.start()
    return copy


def gather_kernel(own_ref, table_ref, own_sem, cross_s, cross_r, ring_s, ring_r, whole_s, whole_r, pass_s, pass_r):
    z, ylo, x, yhi, core = place()
    me = yhi * 2 + core
    far = (1 - yhi) * 2 + core
    count = own_ref.shape[0]
    third = count // 8
    sibling = device(z, ylo, x, yhi, 1 - core)
    cross = device(z, 1 - ylo, x, 1 - yhi, core)
    x_ring = [device(z, ylo, (x + d) % 4, yhi, core) for d in (1, 2, 3)]
    z_ring = [device((z + d) % 4, ylo, x, yhi, core) for d in (1, 2, 3)]
    greet([sibling, cross] + x_ring + z_ring)

    here = pltpu.make_async_copy(own_ref, table_ref.at[pl.ds(me * count, count)], own_sem)
    here.start()
    copies = []
    first = [x * third, count // 2 + z * third]
    arrivals = {}
    for i in range(third):
        for ring in range(2):
            unit = first[ring] + i
            arrivals[ring, i] = send(
                own_ref.at[unit], table_ref.at[me * count + unit], (cross_s, cross_r), ring * third + i, cross
            )
    copies.append(
        send(own_ref, table_ref.at[pl.ds(me * count, count)], (whole_s, whole_r), 0, sibling)
    )
    rings = (x_ring, z_ring)
    landed = {}
    for i in range(third):
        for ring in range(2):
            arrivals[ring, i].wait()
            slot = far * count + first[ring] + i
            for d in (2, 1, 3):
                landed[ring, d, i] = send(
                    table_ref.at[slot], table_ref.at[slot], (ring_s, ring_r), (ring * 3 + d - 1) * third + i, rings[ring][d - 1]
                )
            copies.append(
                send(table_ref.at[slot], table_ref.at[slot], (pass_s, pass_r), ring * 4 * third + i, sibling)
            )
    for i in range(third):
        for ring in range(2):
            for d in (1, 3, 2):
                landed[ring, d, i].wait()
                axis = (x, z)[ring]
                behind = (axis - d + 4) % 4
                slot = far * count + ring * (count // 2) + behind * third + i
                copies.append(
                    send(table_ref.at[slot], table_ref.at[slot], (pass_s, pass_r), (ring * 4 + d) * third + i, sibling)
                )
    here.wait()
    for copy in copies:
        copy.wait()


def gather_call(own, owners):
    count = own.shape[0]
    third = count // 8
    dma = lambda n: [pltpu.SemaphoreType.DMA((n,))] * 2
    return pl.pallas_call(
        gather_kernel,
        in_specs=[pl.BlockSpec(memory_space=pl.ANY)],
        out_specs=pl.BlockSpec(memory_space=pl.ANY),
        out_shape=jax.ShapeDtypeStruct((owners * count,) + own.shape[1:], own.dtype),
        scratch_shapes=[pltpu.SemaphoreType.DMA] + dma(2 * third) + dma(6 * third) + dma(1) + dma(8 * third),
        compiler_params=pltpu.CompilerParams(collective_id=0, has_side_effects=True),
        name="gather_operators",
    )(own)


def row_of(t):
    return 25 * t // 2


def last_window(s, t):
    if s == 0:
        base, top = 96 * (t // 8) + 48 * ((t // 4) % 2), 48
    elif s == 1:
        base, top = 192 * (t // 16) + 48 * ((t // 4) % 4), 48
    else:
        z = (t // 2) % 4
        base, top = 96 * (t // 8) + 16 * z + 16 * (z // 2), 32
    part = row_of(t) - base
    local = 16 * (part // 16) - 16 * (part // top)
    return base + local, local


def window(start, size):
    return pl.ds(pl.multiple_of(start, 16), size)


def total(out, own, parts):
    value = own.astype(jnp.float32)
    for part in parts:
        value = value + part.astype(jnp.float32)
    out[...] = value.astype(out.dtype)


def reduce_kernel(
    grads_ref, out_ref, own, near,
    a0, b0, c0, a1, b1, c1, a2, b2, c2, m0, n0, m1, n1, m2, n2, own_sem, send_sem, recv_sem,
):
    z, ylo, x, yhi, core = place()
    sems = (send_sem, recv_sem)
    sibling = device(z, ylo, x, yhi, 1 - core)
    z_at = [(z + d) % 4 for d in (1, 2, 3)]
    x_at = [(x + d) % 4 for d in (1, 2, 3)]
    y_at = [(yhi, 1 - ylo), (1 - yhi, ylo), (1 - yhi, 1 - ylo)]
    z_ring = [device(v, ylo, x, yhi, core) for v in z_at]
    x_ring = [device(z, ylo, v, yhi, core) for v in x_at]
    y_ring = [device(z, v, x, h, core) for h, v in y_at]
    greet([sibling] + z_ring + x_ring + y_ring)

    mine, pairs = [], []
    for s in range(3):
        pairs.append(send(grads_ref.at[1 - core, s], near.at[s], sems, s, sibling))
        mine.append(pltpu.make_async_copy(grads_ref.at[core, s], own.at[s], own_sem.at[s]))
        mine[-1].start()

    first = []
    for s in range(3):
        mine[s].wait()
        pairs[s].wait()
        for i in range(4):
            total(own.at[s, i], own[s, i], [near[s, i]])
        for d in range(3):
            if s == 0:
                src = own.at[s, :, window(96 * z_at[d], 112)]
                copy = send(src, a0.at[d], sems, 3 + s * 3 + d, z_ring[d])
            elif s == 1:
                h, v = y_at[d]
                src = own.at[s, pl.ds(2 * h, 2), window(192 * v, 208)]
                copy = send(src, a1.at[d], sems, 3 + s * 3 + d, y_ring[d])
            else:
                src = own.at[s, :, window(96 * x_at[d], 112)]
                copy = send(src, a2.at[d], sems, 3 + s * 3 + d, x_ring[d])
            first.append(copy)

    second = []
    for s in range(3):
        for d in range(3):
            first[s * 3 + d].wait()
        if s == 0:
            total(m0, own[s, :, window(96 * z, 112)], [a0[d] for d in range(3)])
        elif s == 1:
            total(m1, own[s, pl.ds(2 * yhi, 2), window(192 * ylo, 208)], [a1[d] for d in range(3)])
        else:
            total(m2, own[s, :, window(96 * x, 112)], [a2[d] for d in range(3)])
        for d in range(3):
            if s == 0:
                h, v = y_at[d]
                copy = send(m0.at[pl.ds(2 * h, 2), window(48 * v, 64)], b0.at[d], sems, 12 + s * 3 + d, y_ring[d])
            elif s == 1:
                copy = send(m1.at[:, window(48 * x_at[d], 64)], b1.at[d], sems, 12 + s * 3 + d, x_ring[d])
            else:
                v = z_at[d]
                copy = send(m2.at[:, window(16 * v + 16 * (v // 2), 48)], b2.at[d], sems, 12 + s * 3 + d, z_ring[d])
            second.append(copy)

    third = []
    for s in range(3):
        for d in range(3):
            second[s * 3 + d].wait()
        if s == 0:
            total(n0, m0[pl.ds(2 * yhi, 2), window(48 * ylo, 64)], [b0[d] for d in range(3)])
        elif s == 1:
            total(n1, m1[:, window(48 * x, 64)], [b1[d] for d in range(3)])
        else:
            total(n2, m2[:, window(16 * z + 16 * (z // 2), 48)], [b2[d] for d in range(3)])
        for d in range(3):
            if s == 0:
                _, at = last_window(0, z * 8 + ylo * 4 + x_at[d])
                copy = send(n0.at[:, window(at, 32)], c0.at[d], sems, 21 + s * 3 + d, x_ring[d])
            elif s == 1:
                _, at = last_window(1, ylo * 16 + x * 4 + z_at[d])
                copy = send(n1.at[:, window(at, 32)], c1.at[d], sems, 21 + s * 3 + d, z_ring[d])
            else:
                h, v = y_at[d]
                _, at = last_window(2, x * 8 + z * 2 + v)
                copy = send(n2.at[pl.ds(2 * h, 2), window(at, 32)], c2.at[d], sems, 21 + s * 3 + d, y_ring[d])
            third.append(copy)

    for s in range(3):
        for d in range(3):
            third[s * 3 + d].wait()
        if s == 0:
            _, at = last_window(0, z * 8 + ylo * 4 + x)
            total(out_ref.at[s], n0[:, window(at, 32)], [c0[d] for d in range(3)])
        elif s == 1:
            _, at = last_window(1, ylo * 16 + x * 4 + z)
            total(out_ref.at[s], n1[:, window(at, 32)], [c1[d] for d in range(3)])
        else:
            _, at = last_window(2, x * 8 + z * 2 + ylo)
            total(out_ref.at[s], n2[pl.ds(2 * yhi, 2), window(at, 32)], [c2[d] for d in range(3)])


def reduce_call(grads):
    _, _, four, rows, lanes = grads.shape
    buf = lambda *shape: pltpu.VMEM(shape + (lanes,), jnp.bfloat16)
    return pl.pallas_call(
        reduce_kernel,
        in_specs=[pl.BlockSpec(memory_space=pl.ANY)],
        out_specs=pl.BlockSpec(memory_space=pltpu.VMEM),
        out_shape=jax.ShapeDtypeStruct((3, 2, 32, lanes), jnp.float32),
        scratch_shapes=[
            buf(3, four, rows), buf(3, four, rows),
            buf(3, 4, 112), buf(3, 2, 64), buf(3, 2, 32),
            buf(3, 2, 208), buf(3, 2, 64), buf(3, 2, 32),
            buf(3, 4, 112), buf(3, 4, 48), buf(3, 2, 32),
            buf(4, 112), buf(2, 64), buf(2, 208), buf(2, 64), buf(4, 112), buf(4, 48),
            pltpu.SemaphoreType.DMA((3,)), pltpu.SemaphoreType.DMA((30,)), pltpu.SemaphoreType.DMA((30,)),
        ],
        compiler_params=pltpu.CompilerParams(
            collective_id=1, has_side_effects=True, vmem_limit_bytes=VMEM_LIMIT
        ),
        name="reduce_operator_gradients",
    )(grads)


def final_share(pieces, width):
    blk = lax.axis_size("blk")
    place_1 = lambda b: ((b // 4) % 2) * 16 + (b % 4) * 4 + b // 8
    place_2 = lambda b: (b % 4) * 8 + (b // 8) * 2 + (b // 4) % 2
    t = lax.axis_index("blk")
    shares = []
    for s, at in enumerate((None, place_1, place_2)):
        piece = pieces[s, :, :, :width]
        if at is not None:
            piece = lax.ppermute(piece, "blk", [(b, at(b)) for b in range(blk)])
        start, _ = last_window(s, t)
        skip = t * (width * width // blk) - start * width
        flat = piece.reshape(2, 32 * width)
        shares.append(lax.dynamic_slice(flat, (0, skip), (2, width * width // blk)))
    return jnp.concatenate(shares, axis=0)


def from_behind(value, axis, steps):
    count = lax.axis_size(axis)
    pairs = [(source, (source + steps) % count) for source in range(count)]
    return lax.ppermute(value, axis, pairs)


def body(left, left_state, right, right_state, operators, need_list, block_slot, sources, targets, negatives):
    owned_count, width, _ = operators.shape
    owners = lax.axis_size("rel")
    nblk = block_slot.shape[-1]
    nrel = owned_count * owners
    rel = need_list[0].reshape(-1)[block_slot[0].reshape(-1)]
    src = sources[0].reshape(BUCKETS * nblk, 1, -1)
    tgt = targets[0].reshape(BUCKETS * nblk, 1, -1)
    neg = negatives[0].reshape(BUCKETS * nblk, 1, -1)
    padded = UNITS * UNIT_ROWS
    own = jnp.pad(operators, ((0, 0), (0, padded - width), (0, LANES - width)))
    table = gather_call(own.reshape(owned_count * UNITS, UNIT_ROWS, LANES), owners)
    ops = table.reshape(nrel, padded, LANES)
    L, LS, R, RS = left.T, left_state[None], right.T, right_state[None]
    s, q = first_call(rel[:nblk], L, src[:nblk], ops, nblk)
    heads, grads = [s], []
    for t in range(BUCKETS):
        at = slice(nblk * t, nblk * t + nblk)
        p, fresh, fresh_acc = right_call(R, RS, q, tgt[at], neg[at])
        moved = from_behind((fresh, fresh_acc), "blk", 1)
        more = t + 1 < BUCKETS
        both = slice(nblk * t, nblk * (t + (2 if more else 1)))
        out = left_call(rel[both], L, LS, R, p, src[both], ops, more)
        grads.append(out[0])
        L, LS = out[1:3]
        if more:
            heads.append(out[3])
            q = out[4]
        R, RS = moved
    partial = opgrad_call(rel, heads, grads, nrel)
    op_grad = final_share(reduce_call(partial), width)
    return (L.T, LS[0], R.T.astype(jnp.float32), RS[0], op_grad)


def solution(mesh):
    in_specs = (
        P(("blk", "rel"), None),
        P(("blk", "rel")),
        P(("blk", "rel"), None),
        P(("blk", "rel")),
        P("rel", None, None),
        P(("blk", "rel"), None, None),
        P(("blk", "rel"), None, None),
        P(("blk", "rel"), None, None),
        P(("blk", "rel"), None, None),
        P(("blk", "rel"), None, None, None),
    )
    out_specs = (
        P(("blk", "rel"), None),
        P(("blk", "rel")),
        P(("blk", "rel"), None),
        P(("blk", "rel")),
        P("rel", "blk"),
    )
    return jax.shard_map(body, mesh=mesh, in_specs=in_specs, out_specs=out_specs, check_vma=False)
```

```python
import functools
import jax
import jax.numpy as jnp
from jax import lax
from jax.experimental import pallas as pl
from jax.experimental.pallas import tpu as pltpu
from jax.sharding import PartitionSpec as P

BUCKETS = 3
STEP = 0.3
NT = (((1,), (1,)), ((), ()))
TN = (((0,), (0,)), ((), ()))
VMEM_LIMIT = 60 * 1024 * 1024
MESH = pl.DeviceIdType.MESH
UNITS = 4
UNIT_ROWS = 112
LANES = 512
CHUNK = 512


def onehot(index, rows):
    index = index.astype(jnp.int16)
    row = lax.broadcasted_iota(jnp.int16, (rows, index.shape[1]), 0)
    one = jnp.ones((), jnp.bfloat16)
    return jnp.where(row == index, one, jnp.zeros((), jnp.bfloat16))


def dot(a, b, dims=None):
    if dims is None:
        return jnp.dot(a, b, preferred_element_type=jnp.float32)
    return lax.dot_general(a, b, dims, preferred_element_type=jnp.float32)


def place():
    b, r = lax.axis_index("blk"), lax.axis_index("rel")
    return b // 8, (b // 4) % 2, b % 4, r // 2, r % 2


def device(z, ylo, x, yhi, core):
    return (z * 8 + ylo * 4 + x, yhi * 2 + core)


def greet(peers):
    barrier = pltpu.get_barrier_semaphore()
    for peer in peers:
        pl.semaphore_signal(barrier, inc=1, device_id=peer, device_id_type=MESH)
    pl.semaphore_wait(barrier, len(peers))


def remote(src, dst, sems, index, peer):
    return pltpu.make_async_remote_copy(
        src_ref=src,
        dst_ref=dst,
        send_sem=sems[0].at[index],
        recv_sem=sems[1].at[index],
        device_id=peer,
        device_id_type=MESH,
    )


def send(src, dst, sems, index, peer):
    copy = remote(src, dst, sems, index, peer)
    copy.start()
    return copy


def adagrad(rows, acc, grad):
    acc = acc + jnp.sum(grad * grad, axis=0, keepdims=True) * (1.0 / grad.shape[0])
    return rows - STEP * grad * lax.rsqrt(acc), acc


def train_kernel(
    rel_ref, own_ref, left_ref, lacc_ref, right_ref, racc_ref, src_ref, tgt_ref, neg_ref,
    newleft_ref, newlacc_ref, fresh_ref, freshacc_ref, s_ref, g_ref,
    table, half, rhalf, rhalf_t, hot, query, scaled, push, scale, back, count, rows_now, acc_now,
    out_rows, out_acc, in_rows, in_acc,
    cross_s, cross_r, ring_s, ring_r, whole_s, whole_r, pass_s, pass_r, move_s, move_r, acc_s, acc_r,
):
    z, ylo, x, yhi, core = place()
    me = yhi * 2 + core
    far = (1 - yhi) * 2 + core
    width, rows = left_ref.shape
    owned = own_ref.shape[0]
    units = owned * UNITS
    third = units // 8
    edges = src_ref.shape[2]
    block = neg_ref.shape[2]
    nblk = edges // block
    blks, rels = 32, 4
    b, r = lax.axis_index("blk"), lax.axis_index("rel")
    ahead, behind_me = ((b + 1) % blks, r), ((b + blks - 1) % blks, r)
    sibling = device(z, ylo, x, yhi, 1 - core)
    cross = device(z, 1 - ylo, x, 1 - yhi, core)
    x_ring = [device(z, ylo, (x + d) % 4, yhi, core) for d in (1, 2, 3)]
    z_ring = [device((z + d) % 4, ylo, x, yhi, core) for d in (1, 2, 3)]
    greet([sibling, cross, ahead, behind_me] + x_ring + z_ring)

    for j in range(owned):
        for u in range(UNITS):
            size = min(UNIT_ROWS, width - u * UNIT_ROWS)
            slot = me * units + j * UNITS + u
            part = own_ref[j, u * UNIT_ROWS : u * UNIT_ROWS + size, :]
            table[slot] = jnp.pad(part, ((0, UNIT_ROWS - size), (0, LANES - width)))
    first = [x * third, units // 2 + z * third]
    arrivals = {}
    for i in range(third):
        for ring in range(2):
            slot = me * units + first[ring] + i
            arrivals[ring, i] = send(table.at[slot], table.at[slot], (cross_s, cross_r), ring * third + i, cross)
    mine = table.at[pl.ds(me * units, units)]
    copies = [send(mine, mine, (whole_s, whole_r), 0, sibling)]

    def heads(t):
        for c in range(0, edges, CHUNK):
            cols = slice(c, c + CHUNK)
            part = onehot(src_ref[t, :, cols], rows)
            hot[:, cols] = part
            s_ref[t, :, cols] = dot(half[...], part).astype(jnp.bfloat16)

    def counts(t):
        def step(k, carry):
            hits = onehot(neg_ref[t * nblk + k], rows)
            ones = jnp.ones((block, 128), jnp.bfloat16)
            count[t * nblk + k] = (dot(hits, ones) * (1.0 / block)).astype(jnp.bfloat16)
            return carry

        lax.fori_loop(0, nblk, step, 0)

    newleft_ref[...] = left_ref[...]
    newlacc_ref[...] = lacc_ref[...]
    half[...] = left_ref[...].astype(jnp.bfloat16)
    rows_now[...] = right_ref[...]
    acc_now[...] = racc_ref[...]
    heads(0)
    rings = (x_ring, z_ring)
    landed = {}
    for i in range(third):
        for ring in range(2):
            arrivals[ring, i].wait()
            slot = far * units + first[ring] + i
            for d in (2, 1, 3):
                landed[ring, d, i] = send(
                    table.at[slot], table.at[slot], (ring_s, ring_r), (ring * 3 + d - 1) * third + i, rings[ring][d - 1]
                )
            copies.append(
                send(table.at[slot], table.at[slot], (pass_s, pass_r), ring * 4 * third + i, sibling)
            )
        counts(i)
    for i in range(third):
        for ring in range(2):
            for d in (1, 3, 2):
                landed[ring, d, i].wait()
                axis = (x, z)[ring]
                from_axis = (axis - d + 4) % 4
                slot = far * units + ring * (units // 2) + from_axis * third + i
                copies.append(
                    send(table.at[slot], table.at[slot], (pass_s, pass_r), (ring * 4 + d) * third + i, sibling)
                )
    for copy in copies:
        copy.wait()

    def operator(t, k):
        op = table[pl.ds(rel_ref[t * nblk + k] * UNITS, UNITS)]
        return op.reshape(UNITS * UNIT_ROWS, LANES)[:width, :width]

    def moves(t):
        return (
            remote(out_rows.at[t], in_rows.at[t], (move_s, move_r), t, ahead),
            remote(out_acc.at[t], in_acc.at[t], (acc_s, acc_r), t, ahead),
        )

    def bucket(t, carry):
        for k in range(nblk):
            cols = slice(k * block, (k + 1) * block)
            query[:, cols] = dot(operator(t, k), s_ref[t, :, cols], TN).astype(jnp.bfloat16)
        rhalf[...] = rows_now[...].astype(jnp.bfloat16)
        rhalf_t[...] = rhalf[...].T

        def scores(k, carry):
            cols = pl.ds(pl.multiple_of(k * block, block), block)
            q = query[:, cols]
            score = dot(rhalf_t[...], q)
            hit = lax.broadcasted_iota(jnp.int32, (rows, block), 0) == tgt_ref[t, :, cols]
            pos = jnp.sum(jnp.where(hit, score, 0.0), axis=0, keepdims=True)
            pull = jax.nn.sigmoid(-pos)
            size = jnp.maximum(pull, 2.0**-8)
            inverse = 1.0 / size
            times = count[t * nblk + k].astype(jnp.float32)
            times = jnp.concatenate([times] * (block // 128), axis=1)
            sig = (0.5 * inverse) * jnp.tanh(0.5 * score) + 0.5 * inverse
            push[:, cols] = (sig * times - jnp.where(hit, pull * inverse, 0.0)).astype(jnp.bfloat16)
            scale[:, cols] = size
            scaled[:, cols] = (q.astype(jnp.float32) * size).astype(jnp.bfloat16)
            return carry

        lax.fori_loop(0, nblk, scores, 0)
        fresh, acc = adagrad(rows_now[...], acc_now[...], dot(scaled[...], push[...], NT))
        fresh = fresh.astype(jnp.bfloat16)

        @pl.when(t < BUCKETS - 1)
        def _():
            out_rows[t] = fresh
            out_acc[t] = acc
            for move in moves(t):
                move.start()

        @pl.when(t == BUCKETS - 1)
        def _():
            fresh_ref[...] = fresh
            freshacc_ref[...] = acc

        for c in range(0, edges, CHUNK):
            cols = slice(c, c + CHUNK)
            g_ref[t, :, cols] = (dot(rhalf[...], push[:, cols]) * scale[:, cols]).astype(jnp.bfloat16)
        for k in range(nblk):
            cols = slice(k * block, (k + 1) * block)
            back[:, cols] = dot(operator(t, k), g_ref[t, :, cols]).astype(jnp.bfloat16)
        left, acc = adagrad(newleft_ref[...], newlacc_ref[...], dot(back[...], hot[...], NT))
        newleft_ref[...] = left
        newlacc_ref[...] = acc
        half[...] = left.astype(jnp.bfloat16)

        @pl.when(t < BUCKETS - 1)
        def _():
            heads(t + 1)
            for move in moves(t):
                move.wait()
            rows_now[...] = in_rows[t].astype(jnp.float32)
            acc_now[...] = in_acc[t]

        return carry

    lax.fori_loop(0, BUCKETS, bucket, 0)


def train_call(rel, own, left, lacc, right, racc, src, tgt, neg):
    width, rows = left.shape
    owned = own.shape[0]
    units = owned * UNITS
    third = units // 8
    buckets, _, edges = src.shape
    dma = lambda n: [pltpu.SemaphoreType.DMA((n,))] * 2
    vmem = pl.BlockSpec(memory_space=pltpu.VMEM)
    f32, bf16 = jnp.float32, jnp.bfloat16
    return pl.pallas_call(
        train_kernel,
        in_specs=[pl.BlockSpec(memory_space=pltpu.SMEM)] + [vmem] * 8,
        out_specs=[vmem] * 6,
        out_shape=[
            jax.ShapeDtypeStruct((width, rows), f32),
            jax.ShapeDtypeStruct((1, rows), f32),
            jax.ShapeDtypeStruct((width, rows), bf16),
            jax.ShapeDtypeStruct((1, rows), f32),
            jax.ShapeDtypeStruct((buckets, width, edges), bf16),
            jax.ShapeDtypeStruct((buckets, width, edges), bf16),
        ],
        scratch_shapes=[
            pltpu.VMEM((4 * units, UNIT_ROWS, LANES), bf16),
            pltpu.VMEM((width, rows), bf16),
            pltpu.VMEM((width, rows), bf16),
            pltpu.VMEM((rows, width), bf16),
            pltpu.VMEM((rows, edges), bf16),
            pltpu.VMEM((width, edges), bf16),
            pltpu.VMEM((width, edges), bf16),
            pltpu.VMEM((rows, edges), bf16),
            pltpu.VMEM((1, edges), f32),
            pltpu.VMEM((width, edges), bf16),
            pltpu.VMEM((neg.shape[0], rows, 128), bf16),
            pltpu.VMEM((width, rows), f32),
            pltpu.VMEM((1, rows), f32),
            pltpu.VMEM((buckets - 1, width, rows), bf16),
            pltpu.VMEM((buckets - 1, 1, rows), f32),
            pltpu.VMEM((buckets - 1, width, rows), bf16),
            pltpu.VMEM((buckets - 1, 1, rows), f32),
        ]
        + dma(2 * third) + dma(6 * third) + dma(1) + dma(8 * third) + dma(buckets - 1) + dma(buckets - 1),
        compiler_params=pltpu.CompilerParams(
            collective_id=0, has_side_effects=True, vmem_limit_bytes=VMEM_LIMIT
        ),
        name="train_buckets",
    )(rel, own, left, lacc, right, racc, src, tgt, neg)


def opgrad_kernel(nrel, rel_ref, s_ref, g_ref, out_ref, acc_ref, count_ref, list_ref):
    core, part = pl.program_id(0), pl.program_id(1)
    _, width, edges = s_ref.shape
    nblk = rel_ref.shape[0] // 3
    block = edges // nblk

    @pl.when((core == 0) & (part == 0))
    def _():
        def clear(j, carry):
            for t in range(3):
                count_ref[t, j] = 0
            return carry

        lax.fori_loop(0, nrel, clear, 0)
        for t in range(3):
            def note(k, carry):
                j = rel_ref[t * nblk + k]
                n = count_ref[t, j]
                list_ref[t, j * nblk + n] = k
                count_ref[t, j] = n + 1
                return carry

            lax.fori_loop(0, nblk, note, 0)

    for i in range(4):
        j = ((i // 2) * 2 + core) * 6 + part * 2 + i % 2
        acc_ref[...] = jnp.zeros_like(acc_ref)
        for t in range(3):
            def add(n, carry):
                k = list_ref[t, j * nblk + n]
                cols = pl.ds(pl.multiple_of(k * block, block), block)
                acc_ref[...] += dot(s_ref[t, :, cols], g_ref[t, :, cols], NT)
                return carry

            lax.fori_loop(0, count_ref[t, j], add, 0)
        out_ref[0, 0, i, :, :width] = acc_ref[...].astype(jnp.bfloat16)
        out_ref[0, 0, i, :, width:] = jnp.zeros((width, out_ref.shape[-1] - width), jnp.bfloat16)


def opgrad_call(rel, s, g, nrel):
    _, width, edges = s.shape
    nblk = rel.shape[0] // 3
    whole = pl.BlockSpec(s.shape, lambda c, p, rel: (0, 0, 0))
    return pl.pallas_call(
        functools.partial(opgrad_kernel, nrel),
        grid_spec=pltpu.PrefetchScalarGridSpec(
            num_scalar_prefetch=1,
            grid=(2, 3),
            in_specs=[whole] * 2,
            out_specs=pl.BlockSpec((1, 1, 4, width, 512), lambda c, p, rel: (c, p, 0, 0, 0)),
            scratch_shapes=[
                pltpu.VMEM((width, width), jnp.float32),
                pltpu.SMEM((3, nrel), jnp.int32),
                pltpu.SMEM((3, nrel * nblk), jnp.int32),
            ],
        ),
        out_shape=jax.ShapeDtypeStruct((2, 3, 4, width, 512), jnp.bfloat16),
        compiler_params=pltpu.CompilerParams(vmem_limit_bytes=VMEM_LIMIT),
        name="operator_gradients",
    )(rel, s, g)


def row_of(t):
    return 25 * t // 2


def last_window(s, t):
    if s == 0:
        base, top = 96 * (t // 8) + 48 * ((t // 4) % 2), 48
    elif s == 1:
        base, top = 192 * (t // 16) + 48 * ((t // 4) % 4), 48
    else:
        z = (t // 2) % 4
        base, top = 96 * (t // 8) + 16 * z + 16 * (z // 2), 32
    part = row_of(t) - base
    local = 16 * (part // 16) - 16 * (part // top)
    return base + local, local


def window(start, size):
    return pl.ds(pl.multiple_of(start, 16), size)


def total(out, own, parts):
    value = own.astype(jnp.float32)
    for part in parts:
        value = value + part.astype(jnp.float32)
    out[...] = value.astype(out.dtype)


def reduce_kernel(
    grads_ref, out_ref, own, near,
    a0, b0, c0, a1, b1, c1, a2, b2, c2, m0, n0, m1, n1, m2, n2, own_sem, send_sem, recv_sem,
):
    z, ylo, x, yhi, core = place()
    sems = (send_sem, recv_sem)
    sibling = device(z, ylo, x, yhi, 1 - core)
    z_at = [(z + d) % 4 for d in (1, 2, 3)]
    x_at = [(x + d) % 4 for d in (1, 2, 3)]
    y_at = [(yhi, 1 - ylo), (1 - yhi, ylo), (1 - yhi, 1 - ylo)]
    z_ring = [device(v, ylo, x, yhi, core) for v in z_at]
    x_ring = [device(z, ylo, v, yhi, core) for v in x_at]
    y_ring = [device(z, v, x, h, core) for h, v in y_at]
    greet([sibling] + z_ring + x_ring + y_ring)

    mine, pairs = [], []
    for s in range(3):
        pairs.append(send(grads_ref.at[1 - core, s], near.at[s], sems, s, sibling))
        mine.append(pltpu.make_async_copy(grads_ref.at[core, s], own.at[s], own_sem.at[s]))
        mine[-1].start()

    first = []
    for s in range(3):
        mine[s].wait()
        pairs[s].wait()
        for i in range(4):
            total(own.at[s, i], own[s, i], [near[s, i]])
        for d in range(3):
            if s == 0:
                src = own.at[s, :, window(96 * z_at[d], 112)]
                copy = send(src, a0.at[d], sems, 3 + s * 3 + d, z_ring[d])
            elif s == 1:
                h, v = y_at[d]
                src = own.at[s, pl.ds(2 * h, 2), window(192 * v, 208)]
                copy = send(src, a1.at[d], sems, 3 + s * 3 + d, y_ring[d])
            else:
                src = own.at[s, :, window(96 * x_at[d], 112)]
                copy = send(src, a2.at[d], sems, 3 + s * 3 + d, x_ring[d])
            first.append(copy)

    second = []
    for s in range(3):
        for d in range(3):
            first[s * 3 + d].wait()
        if s == 0:
            total(m0, own[s, :, window(96 * z, 112)], [a0[d] for d in range(3)])
        elif s == 1:
            total(m1, own[s, pl.ds(2 * yhi, 2), window(192 * ylo, 208)], [a1[d] for d in range(3)])
        else:
            total(m2, own[s, :, window(96 * x, 112)], [a2[d] for d in range(3)])
        for d in range(3):
            if s == 0:
                h, v = y_at[d]
                copy = send(m0.at[pl.ds(2 * h, 2), window(48 * v, 64)], b0.at[d], sems, 12 + s * 3 + d, y_ring[d])
            elif s == 1:
                copy = send(m1.at[:, window(48 * x_at[d], 64)], b1.at[d], sems, 12 + s * 3 + d, x_ring[d])
            else:
                v = z_at[d]
                copy = send(m2.at[:, window(16 * v + 16 * (v // 2), 48)], b2.at[d], sems, 12 + s * 3 + d, z_ring[d])
            second.append(copy)

    third = []
    for s in range(3):
        for d in range(3):
            second[s * 3 + d].wait()
        if s == 0:
            total(n0, m0[pl.ds(2 * yhi, 2), window(48 * ylo, 64)], [b0[d] for d in range(3)])
        elif s == 1:
            total(n1, m1[:, window(48 * x, 64)], [b1[d] for d in range(3)])
        else:
            total(n2, m2[:, window(16 * z + 16 * (z // 2), 48)], [b2[d] for d in range(3)])
        for d in range(3):
            if s == 0:
                _, at = last_window(0, z * 8 + ylo * 4 + x_at[d])
                copy = send(n0.at[:, window(at, 32)], c0.at[d], sems, 21 + s * 3 + d, x_ring[d])
            elif s == 1:
                _, at = last_window(1, ylo * 16 + x * 4 + z_at[d])
                copy = send(n1.at[:, window(at, 32)], c1.at[d], sems, 21 + s * 3 + d, z_ring[d])
            else:
                h, v = y_at[d]
                _, at = last_window(2, x * 8 + z * 2 + v)
                copy = send(n2.at[pl.ds(2 * h, 2), window(at, 32)], c2.at[d], sems, 21 + s * 3 + d, y_ring[d])
            third.append(copy)

    for s in range(3):
        for d in range(3):
            third[s * 3 + d].wait()
        if s == 0:
            _, at = last_window(0, z * 8 + ylo * 4 + x)
            total(out_ref.at[s], n0[:, window(at, 32)], [c0[d] for d in range(3)])
        elif s == 1:
            _, at = last_window(1, ylo * 16 + x * 4 + z)
            total(out_ref.at[s], n1[:, window(at, 32)], [c1[d] for d in range(3)])
        else:
            _, at = last_window(2, x * 8 + z * 2 + ylo)
            total(out_ref.at[s], n2[pl.ds(2 * yhi, 2), window(at, 32)], [c2[d] for d in range(3)])


def reduce_call(grads):
    _, _, four, rows, lanes = grads.shape
    buf = lambda *shape: pltpu.VMEM(shape + (lanes,), jnp.bfloat16)
    return pl.pallas_call(
        reduce_kernel,
        in_specs=[pl.BlockSpec(memory_space=pl.ANY)],
        out_specs=pl.BlockSpec(memory_space=pltpu.VMEM),
        out_shape=jax.ShapeDtypeStruct((3, 2, 32, lanes), jnp.float32),
        scratch_shapes=[
            buf(3, four, rows), buf(3, four, rows),
            buf(3, 4, 112), buf(3, 2, 64), buf(3, 2, 32),
            buf(3, 2, 208), buf(3, 2, 64), buf(3, 2, 32),
            buf(3, 4, 112), buf(3, 4, 48), buf(3, 2, 32),
            buf(4, 112), buf(2, 64), buf(2, 208), buf(2, 64), buf(4, 112), buf(4, 48),
            pltpu.SemaphoreType.DMA((3,)), pltpu.SemaphoreType.DMA((30,)), pltpu.SemaphoreType.DMA((30,)),
        ],
        compiler_params=pltpu.CompilerParams(
            collective_id=1, has_side_effects=True, vmem_limit_bytes=VMEM_LIMIT
        ),
        name="reduce_operator_gradients",
    )(grads)


def final_share(pieces, width):
    blk = lax.axis_size("blk")
    place_1 = lambda b: ((b // 4) % 2) * 16 + (b % 4) * 4 + b // 8
    place_2 = lambda b: (b % 4) * 8 + (b // 8) * 2 + (b // 4) % 2
    t = lax.axis_index("blk")
    shares = []
    for s, at in enumerate((None, place_1, place_2)):
        piece = pieces[s, :, :, :width]
        if at is not None:
            piece = lax.ppermute(piece, "blk", [(b, at(b)) for b in range(blk)])
        start, _ = last_window(s, t)
        skip = t * (width * width // blk) - start * width
        flat = piece.reshape(2, 32 * width)
        shares.append(lax.dynamic_slice(flat, (0, skip), (2, width * width // blk)))
    return jnp.concatenate(shares, axis=0)


def from_behind(value, axis, steps):
    count = lax.axis_size(axis)
    pairs = [(source, (source + steps) % count) for source in range(count)]
    return lax.ppermute(value, axis, pairs)


def body(left, left_state, right, right_state, operators, need_list, block_slot, sources, targets, negatives):
    owned_count, width, _ = operators.shape
    owners = lax.axis_size("rel")
    nrel = owned_count * owners
    rel = need_list[0].reshape(-1)[block_slot[0].reshape(-1)]
    src = sources[0][:, None]
    tgt = targets[0][:, None]
    neg = negatives[0].reshape(-1, 1, negatives.shape[-1])
    L, LS, R, RS, s, g = train_call(
        rel, operators, left.T, left_state[None], right.T, right_state[None], src, tgt, neg
    )
    R, RS = from_behind((R, RS), "blk", 1)
    op_grad = final_share(reduce_call(opgrad_call(rel, s, g, nrel)), width)
    return (L.T, LS[0], R.T.astype(jnp.float32), RS[0], op_grad)


def solution(mesh):
    in_specs = (
        P(("blk", "rel"), None),
        P(("blk", "rel")),
        P(("blk", "rel"), None),
        P(("blk", "rel")),
        P("rel", None, None),
        P(("blk", "rel"), None, None),
        P(("blk", "rel"), None, None),
        P(("blk", "rel"), None, None),
        P(("blk", "rel"), None, None),
        P(("blk", "rel"), None, None, None),
    )
    out_specs = (
        P(("blk", "rel"), None),
        P(("blk", "rel")),
        P(("blk", "rel"), None),
        P(("blk", "rel")),
        P("rel", "blk"),
    )
    return jax.shard_map(body, mesh=mesh, in_specs=in_specs, out_specs=out_specs, check_vma=False)
```

```python
import functools
import jax
import jax.numpy as jnp
from jax import lax
from jax.experimental import pallas as pl
from jax.experimental.pallas import tpu as pltpu
from jax.sharding import PartitionSpec as P

BUCKETS = 3
STEP = 0.3
NT = (((1,), (1,)), ((), ()))
TN = (((0,), (0,)), ((), ()))
VMEM_LIMIT = 60 * 1024 * 1024
MESH = pl.DeviceIdType.MESH
UNITS = 4
LANES = 512
CHUNK = 512


def onehot(index, rows):
    index = index.astype(jnp.int16)
    row = lax.broadcasted_iota(jnp.int16, (rows, index.shape[1]), 0)
    one = jnp.ones((), jnp.bfloat16)
    return jnp.where(row == index, one, jnp.zeros((), jnp.bfloat16))


def dot(a, b, dims=None):
    if dims is None:
        return jnp.dot(a, b, preferred_element_type=jnp.float32)
    return lax.dot_general(a, b, dims, preferred_element_type=jnp.float32)


def place():
    b, r = lax.axis_index("blk"), lax.axis_index("rel")
    return b // 8, (b // 4) % 2, b % 4, r // 2, r % 2


def device(z, ylo, x, yhi, core):
    return (z * 8 + ylo * 4 + x, yhi * 2 + core)


def greet(peers):
    barrier = pltpu.get_barrier_semaphore()
    for peer in peers:
        pl.semaphore_signal(barrier, inc=1, device_id=peer, device_id_type=MESH)
    pl.semaphore_wait(barrier, len(peers))


def remote(src, dst, sems, index, peer):
    return pltpu.make_async_remote_copy(
        src_ref=src,
        dst_ref=dst,
        send_sem=sems[0].at[index],
        recv_sem=sems[1].at[index],
        device_id=peer,
        device_id_type=MESH,
    )


def send(src, dst, sems, index, peer):
    copy = remote(src, dst, sems, index, peer)
    copy.start()
    return copy


def adagrad(rows, acc, grad):
    acc = acc + jnp.sum(grad * grad, axis=0, keepdims=True) * (1.0 / grad.shape[0])
    return rows - STEP * grad * lax.rsqrt(acc), acc


def train_kernel(
    info_ref, own_ref, left_ref, lacc_ref, right_ref, racc_ref, src_ref, tgt_ref, neg_ref,
    newleft_ref, newlacc_ref, newright_ref, newracc_ref, grads_ref, near_ref,
    table, fresh_ref, freshacc_ref, half, rhalf, rhalf_t, hot, query, scaled, heads_now, push, scale, score, count, sums, rows_now, acc_now,
    in_rows, in_acc, load_sem, store_sem,
    cross_s, cross_r, ring_s, ring_r, whole_s, whole_r, pass_s, pass_r, move_s, move_r, acc_s, acc_r, near_s, near_r,
):
    z, ylo, x, yhi, core = place()
    me = yhi * 2 + core
    far = (1 - yhi) * 2 + core
    width, rows = newleft_ref.shape
    owned = own_ref.shape[0]
    units = owned * UNITS
    third = units // 8
    edges = src_ref.shape[2]
    block = neg_ref.shape[2]
    nblk = edges // block
    nrel = table.shape[0]
    total_blocks = BUCKETS * nblk
    blks = 32
    b, r = lax.axis_index("blk"), lax.axis_index("rel")
    ahead, behind = ((b + 1) % blks, r), ((b + blks - 1) % blks, r)
    sibling = device(z, ylo, x, yhi, 1 - core)
    cross = device(z, 1 - ylo, x, 1 - yhi, core)
    x_ring = [device(z, ylo, (x + d) % 4, yhi, core) for d in (1, 2, 3)]
    z_ring = [device((z + d) % 4, ylo, x, yhi, core) for d in (1, 2, 3)]
    loads = [
        pltpu.make_async_copy(left_ref, newleft_ref, load_sem.at[0]),
        pltpu.make_async_copy(right_ref, rows_now, load_sem.at[1]),
    ]
    for load in loads:
        load.start()
    greet([sibling, cross, ahead, behind] + x_ring + z_ring)

    for j in range(owned):
        table[me * owned + j] = jnp.pad(own_ref[j], ((0, 0), (0, LANES - width)))

    def unit(owner, u):
        lanes = LANES // UNITS
        return table.at[owner * owned + u // UNITS, :, pl.ds(pl.multiple_of((u % UNITS) * lanes, lanes), lanes)]

    first = [x * third, units // 2 + z * third]
    arrivals = {}
    for i in range(third):
        for ring in range(2):
            part = unit(me, first[ring] + i)
            arrivals[ring, i] = send(part, part, (cross_s, cross_r), ring * third + i, cross)
    mine = table.at[pl.ds(me * owned, owned)]
    copies = [send(mine, mine, (whole_s, whole_r), 0, sibling)]

    def heads(t):
        for c in range(0, edges, CHUNK):
            cols = slice(c, c + CHUNK)
            hot[:, cols] = onehot(src_ref[t, :, cols], rows)
            heads_now[:, cols] = dot(half[...], hot[:, cols]).astype(jnp.bfloat16)

    def counts(t):
        def step(k, carry):
            hits = onehot(neg_ref[t * nblk + k], rows)
            ones = jnp.ones((block, 128), jnp.bfloat16)
            count[k] = (dot(hits, ones) * (1.0 / block)).astype(jnp.bfloat16)
            return carry

        lax.fori_loop(0, nblk, step, 0)

    def clear(n, carry):
        sums[n] = jnp.zeros(sums.shape[1:], jnp.float32)
        return carry

    newlacc_ref[...] = lacc_ref[...]
    acc_now[...] = racc_ref[...]
    for load in loads:
        load.wait()
    half[...] = newleft_ref[...].astype(jnp.bfloat16)
    heads(0)
    rings = (x_ring, z_ring)
    landed = {}
    for i in range(third):
        for ring in range(2):
            arrivals[ring, i].wait()
            part = unit(far, first[ring] + i)
            for d in (2, 1, 3):
                landed[ring, d, i] = send(
                    part, part, (ring_s, ring_r), (ring * 3 + d - 1) * third + i, rings[ring][d - 1]
                )
            copies.append(send(part, part, (pass_s, pass_r), ring * 4 * third + i, sibling))
        if i == 0:
            counts(0)
        elif i == 1:
            lax.fori_loop(0, sums.shape[0], clear, 0)
    for i in range(third):
        for ring in range(2):
            for d in (1, 3, 2):
                landed[ring, d, i].wait()
                origin = ((x, z)[ring] - d + 4) % 4
                part = unit(far, ring * (units // 2) + origin * third + i)
                copies.append(send(part, part, (pass_s, pass_r), (ring * 4 + d) * third + i, sibling))
    for copy in copies:
        copy.wait()

    def operator(t, k):
        return table[info_ref[t * nblk + k]][:, :width]

    def earlier(n):
        return jnp.where(n < total_blocks, sums[jnp.minimum(n, total_blocks - 1)], 0.0)

    def moves(t):
        return (
            remote(fresh_ref, in_rows.at[t], (move_s, move_r), t, ahead),
            remote(freshacc_ref, in_acc.at[t], (acc_s, acc_r), t, ahead),
        )

    last_moves = (
        remote(fresh_ref, newright_ref, (move_s, move_r), BUCKETS - 1, ahead),
        remote(freshacc_ref, newracc_ref, (acc_s, acc_r), BUCKETS - 1, ahead),
    )

    def bucket(t, carry):
        for k in range(nblk):
            cols = slice(k * block, (k + 1) * block)
            query[:, cols] = dot(operator(t, k), heads_now[:, cols], TN).astype(jnp.bfloat16)
        rhalf[...] = rows_now[...].astype(jnp.bfloat16)
        rhalf_t[...] = rhalf[...].T

        def meet(k, slot):
            cols = pl.ds(pl.multiple_of(k * block, block), block)
            value = dot(rhalf_t[...], query[:, cols])
            score[slot] = value
            hit = lax.broadcasted_iota(jnp.int32, (rows, block), 0) == tgt_ref[t, :, cols]
            pos = jnp.sum(jnp.where(hit, value, 0.0), axis=0, keepdims=True)
            scale[:, cols] = jax.nn.sigmoid(-pos)

        def weigh(k, slot):
            cols = pl.ds(pl.multiple_of(k * block, block), block)
            pull = scale[:, cols]
            size = jnp.maximum(pull, 2.0**-8)
            inverse = 1.0 / size
            times = jnp.concatenate([count[k]] * (block // 128), axis=1)
            twice = (jnp.tanh(0.5 * score[slot]) + 1.0).astype(jnp.bfloat16)
            hit = onehot(tgt_ref[t, :, cols], rows)
            push[:, cols] = twice * (0.5 * inverse).astype(jnp.bfloat16) * times - hit * (pull * inverse).astype(
                jnp.bfloat16
            )
            scale[:, cols] = size
            scaled[:, cols] = (query[:, cols].astype(jnp.float32) * size).astype(jnp.bfloat16)

        def two(j, carry):
            meet(2 * j + 1, 1)
            weigh(2 * j, 0)
            meet(2 * j + 2, 0)
            weigh(2 * j + 1, 1)
            return carry

        meet(0, 0)
        lax.fori_loop(0, nblk // 2 - 1, two, 0)
        meet(nblk - 1, 1)
        weigh(nblk - 2, 0)
        weigh(nblk - 1, 1)
        for c in range(0, rows, CHUNK):
            part = slice(c, c + CHUNK)
            fresh, acc = adagrad(rows_now[:, part], acc_now[:, part], dot(scaled[...], push[part, :], NT))
            fresh_ref[:, part] = fresh.astype(jnp.bfloat16)
            freshacc_ref[:, part] = acc

        @pl.when(t < BUCKETS - 1)
        def _():
            for move in moves(t):
                move.start()

        @pl.when(t == BUCKETS - 1)
        def _():
            for move in last_moves:
                move.start()

        for c in range(0, edges, CHUNK):
            cols = slice(c, c + CHUNK)
            scaled[:, cols] = (dot(rhalf[...], push[:, cols]) * scale[:, cols]).astype(jnp.bfloat16)
        for k in range(nblk):
            cols = slice(k * block, (k + 1) * block)
            query[:, cols] = dot(operator(t, k), scaled[:, cols]).astype(jnp.bfloat16)
        for c in range(0, rows, CHUNK):
            part = slice(c, c + CHUNK)
            left, acc = adagrad(newleft_ref[:, part], newlacc_ref[:, part], dot(query[...], hot[part, :], NT))
            newleft_ref[:, part] = left
            newlacc_ref[:, part] = acc
            half[:, part] = left.astype(jnp.bfloat16)
        for k in range(nblk):
            cols = slice(k * block, (k + 1) * block)
            before = earlier(info_ref[total_blocks + t * nblk + k])
            sums[t * nblk + k] = before + dot(heads_now[:, cols], scaled[:, cols], NT)

        @pl.when(t < BUCKETS - 1)
        def _():
            heads(t + 1)
            counts(t + 1)
            for move in moves(t):
                move.wait()
            rows_now[...] = in_rows[t].astype(jnp.float32)
            acc_now[...] = in_acc[t]

        return carry

    lax.fori_loop(0, BUCKETS, bucket, 0)

    copies = []
    for here in (False, True):
        for n in range(nrel // 2):
            part, h, i = n // 4, n // 2 % 2, n % 2
            j = (h * 2 + (core if here else 1 - core)) * owned + part * 2 + i
            table[j, :, :width] = earlier(info_ref[2 * total_blocks + j]).astype(jnp.bfloat16)
            if here:
                copy = pltpu.make_async_copy(table.at[j], grads_ref.at[part, h * 2 + i], store_sem.at[n])
                copy.start()
            else:
                copy = send(table.at[j], near_ref.at[part, h * 2 + i], (near_s, near_r), n, sibling)
            copies.append(copy)
    for copy in copies:
        copy.wait()
    for move in last_moves:
        move.wait()


def train_call(info, own, left, lacc, right, racc, src, tgt, neg, nrel):
    width, rows = left.shape
    owned = own.shape[0]
    units = owned * UNITS
    third = units // 8
    buckets, _, edges = src.shape
    nblk = neg.shape[0] // buckets
    dma = lambda n: [pltpu.SemaphoreType.DMA((n,))] * 2
    vmem = pl.BlockSpec(memory_space=pltpu.VMEM)
    anywhere = pl.BlockSpec(memory_space=pl.ANY)
    f32, bf16 = jnp.float32, jnp.bfloat16
    return pl.pallas_call(
        train_kernel,
        in_specs=[pl.BlockSpec(memory_space=pltpu.SMEM), vmem, anywhere, vmem, anywhere] + [vmem] * 4,
        out_specs=[vmem] * 2 + [anywhere] * 4,
        out_shape=[
            jax.ShapeDtypeStruct((width, rows), f32),
            jax.ShapeDtypeStruct((1, rows), f32),
            jax.ShapeDtypeStruct((width, rows), bf16),
            jax.ShapeDtypeStruct((1, rows), f32),
            jax.ShapeDtypeStruct((3, nrel // 6, width, LANES), bf16),
            jax.ShapeDtypeStruct((3, nrel // 6, width, LANES), bf16),
        ],
        scratch_shapes=[
            pltpu.VMEM((nrel, width, LANES), bf16),
            pltpu.VMEM((width, rows), bf16),
            pltpu.VMEM((1, rows), f32),
            pltpu.VMEM((width, rows), bf16),
            pltpu.VMEM((width, rows), bf16),
            pltpu.VMEM((rows, width), bf16),
            pltpu.VMEM((rows, edges), bf16),
            pltpu.VMEM((width, edges), bf16),
            pltpu.VMEM((width, edges), bf16),
            pltpu.VMEM((width, edges), bf16),
            pltpu.VMEM((rows, edges), bf16),
            pltpu.VMEM((1, edges), f32),
            pltpu.VMEM((2, rows, edges // nblk), f32),
            pltpu.VMEM((nblk, rows, 128), bf16),
            pltpu.VMEM((neg.shape[0], width, width), f32),
            pltpu.VMEM((width, rows), f32),
            pltpu.VMEM((1, rows), f32),
            pltpu.VMEM((buckets - 1, width, rows), bf16),
            pltpu.VMEM((buckets - 1, 1, rows), f32),
            pltpu.SemaphoreType.DMA((2,)),
            pltpu.SemaphoreType.DMA((nrel // 2,)),
        ]
        + dma(2 * third) + dma(6 * third) + dma(1) + dma(8 * third) + dma(buckets) + dma(buckets) + dma(nrel // 2),
        compiler_params=pltpu.CompilerParams(
            collective_id=0, has_side_effects=True, vmem_limit_bytes=VMEM_LIMIT
        ),
        name="train_buckets",
    )(info, own, left, lacc, right, racc, src, tgt, neg)


def row_of(t):
    return 25 * t // 2


def last_window(s, t):
    if s == 0:
        base, top = 96 * (t // 8) + 48 * ((t // 4) % 2), 48
    elif s == 1:
        base, top = 192 * (t // 16) + 48 * ((t // 4) % 4), 48
    else:
        z = (t // 2) % 4
        base, top = 96 * (t // 8) + 16 * z + 16 * (z // 2), 32
    part = row_of(t) - base
    local = 16 * (part // 16) - 16 * (part // top)
    return base + local, local


def window(start, size):
    return pl.ds(pl.multiple_of(start, 16), size)


def total(out, own, parts):
    value = own.astype(jnp.float32)
    for part in parts:
        value = value + part.astype(jnp.float32)
    out[...] = value.astype(out.dtype)


def reduce_kernel(
    grads_ref, near_ref, out_ref, own, near,
    a0, b0, c0, a1, b1, c1, a2, b2, c2, m0, n0, m1, n1, m2, n2, own_sem, near_sem, send_sem, recv_sem,
):
    z, ylo, x, yhi, core = place()
    sems = (send_sem, recv_sem)
    z_at = [(z + d) % 4 for d in (1, 2, 3)]
    x_at = [(x + d) % 4 for d in (1, 2, 3)]
    y_at = [(yhi, 1 - ylo), (1 - yhi, ylo), (1 - yhi, 1 - ylo)]
    z_ring = [device(v, ylo, x, yhi, core) for v in z_at]
    x_ring = [device(z, ylo, v, yhi, core) for v in x_at]
    y_ring = [device(z, v, x, h, core) for h, v in y_at]
    mine, pairs = [], []
    for s in range(3):
        pairs.append(pltpu.make_async_copy(near_ref.at[s], near.at[s], near_sem.at[s]))
        mine.append(pltpu.make_async_copy(grads_ref.at[s], own.at[s], own_sem.at[s]))
        pairs[-1].start()
        mine[-1].start()
    greet(z_ring + x_ring + y_ring)

    first = []
    for s in range(3):
        mine[s].wait()
        pairs[s].wait()
        for i in range(4):
            total(own.at[s, i], own[s, i], [near[s, i]])
        for d in range(3):
            if s == 0:
                src = own.at[s, :, window(96 * z_at[d], 112)]
                copy = send(src, a0.at[d], sems, 3 + s * 3 + d, z_ring[d])
            elif s == 1:
                h, v = y_at[d]
                src = own.at[s, pl.ds(2 * h, 2), window(192 * v, 208)]
                copy = send(src, a1.at[d], sems, 3 + s * 3 + d, y_ring[d])
            else:
                src = own.at[s, :, window(96 * x_at[d], 112)]
                copy = send(src, a2.at[d], sems, 3 + s * 3 + d, x_ring[d])
            first.append(copy)

    second = []
    for s in range(3):
        for d in range(3):
            first[s * 3 + d].wait()
        if s == 0:
            total(m0, own[s, :, window(96 * z, 112)], [a0[d] for d in range(3)])
        elif s == 1:
            total(m1, own[s, pl.ds(2 * yhi, 2), window(192 * ylo, 208)], [a1[d] for d in range(3)])
        else:
            total(m2, own[s, :, window(96 * x, 112)], [a2[d] for d in range(3)])
        for d in range(3):
            if s == 0:
                h, v = y_at[d]
                copy = send(m0.at[pl.ds(2 * h, 2), window(48 * v, 64)], b0.at[d], sems, 12 + s * 3 + d, y_ring[d])
            elif s == 1:
                copy = send(m1.at[:, window(48 * x_at[d], 64)], b1.at[d], sems, 12 + s * 3 + d, x_ring[d])
            else:
                v = z_at[d]
                copy = send(m2.at[:, window(16 * v + 16 * (v // 2), 48)], b2.at[d], sems, 12 + s * 3 + d, z_ring[d])
            second.append(copy)

    third = []
    for s in range(3):
        for d in range(3):
            second[s * 3 + d].wait()
        if s == 0:
            total(n0, m0[pl.ds(2 * yhi, 2), window(48 * ylo, 64)], [b0[d] for d in range(3)])
        elif s == 1:
            total(n1, m1[:, window(48 * x, 64)], [b1[d] for d in range(3)])
        else:
            total(n2, m2[:, window(16 * z + 16 * (z // 2), 48)], [b2[d] for d in range(3)])
        for d in range(3):
            if s == 0:
                _, at = last_window(0, z * 8 + ylo * 4 + x_at[d])
                copy = send(n0.at[:, window(at, 32)], c0.at[d], sems, 21 + s * 3 + d, x_ring[d])
            elif s == 1:
                _, at = last_window(1, ylo * 16 + x * 4 + z_at[d])
                copy = send(n1.at[:, window(at, 32)], c1.at[d], sems, 21 + s * 3 + d, z_ring[d])
            else:
                h, v = y_at[d]
                _, at = last_window(2, x * 8 + z * 2 + v)
                copy = send(n2.at[pl.ds(2 * h, 2), window(at, 32)], c2.at[d], sems, 21 + s * 3 + d, y_ring[d])
            third.append(copy)

    for s in range(3):
        for d in range(3):
            third[s * 3 + d].wait()
        if s == 0:
            _, at = last_window(0, z * 8 + ylo * 4 + x)
            total(out_ref.at[s], n0[:, window(at, 32)], [c0[d] for d in range(3)])
        elif s == 1:
            _, at = last_window(1, ylo * 16 + x * 4 + z)
            total(out_ref.at[s], n1[:, window(at, 32)], [c1[d] for d in range(3)])
        else:
            _, at = last_window(2, x * 8 + z * 2 + ylo)
            total(out_ref.at[s], n2[pl.ds(2 * yhi, 2), window(at, 32)], [c2[d] for d in range(3)])


def reduce_call(grads, near):
    _, four, rows, lanes = grads.shape
    buf = lambda *shape: pltpu.VMEM(shape + (lanes,), jnp.bfloat16)
    return pl.pallas_call(
        reduce_kernel,
        in_specs=[pl.BlockSpec(memory_space=pl.ANY)] * 2,
        out_specs=pl.BlockSpec(memory_space=pltpu.VMEM),
        out_shape=jax.ShapeDtypeStruct((3, 2, 32, lanes), jnp.float32),
        scratch_shapes=[
            buf(3, four, rows), buf(3, four, rows),
            buf(3, 4, 112), buf(3, 2, 64), buf(3, 2, 32),
            buf(3, 2, 208), buf(3, 2, 64), buf(3, 2, 32),
            buf(3, 4, 112), buf(3, 4, 48), buf(3, 2, 32),
            buf(4, 112), buf(2, 64), buf(2, 208), buf(2, 64), buf(4, 112), buf(4, 48),
            pltpu.SemaphoreType.DMA((3,)), pltpu.SemaphoreType.DMA((3,)), pltpu.SemaphoreType.DMA((30,)), pltpu.SemaphoreType.DMA((30,)),
        ],
        compiler_params=pltpu.CompilerParams(
            collective_id=1, has_side_effects=True, vmem_limit_bytes=VMEM_LIMIT
        ),
        name="reduce_operator_gradients",
    )(grads, near)


def final_share(pieces, width):
    blk = lax.axis_size("blk")
    place_1 = lambda b: ((b // 4) % 2) * 16 + (b % 4) * 4 + b // 8
    place_2 = lambda b: (b % 4) * 8 + (b // 8) * 2 + (b // 4) % 2
    t = lax.axis_index("blk")
    shares = []
    for s, at in enumerate((None, place_1, place_2)):
        piece = pieces[s, :, :, :width]
        if at is not None:
            piece = lax.ppermute(piece, "blk", [(b, at(b)) for b in range(blk)])
        start, _ = last_window(s, t)
        skip = t * (width * width // blk) - start * width
        flat = piece.reshape(2, 32 * width)
        shares.append(lax.dynamic_slice(flat, (0, skip), (2, width * width // blk)))
    return jnp.concatenate(shares, axis=0)


def body(left, left_state, right, right_state, operators, need_list, block_slot, sources, targets, negatives):
    owned_count, width, _ = operators.shape
    owners = lax.axis_size("rel")
    nrel = owned_count * owners
    rel = need_list[0].reshape(-1)[block_slot[0].reshape(-1)]
    blocks = rel.shape[0]
    at = jnp.arange(blocks, dtype=jnp.int32)
    latest = lambda found: jnp.max(jnp.where(found, at, -1), axis=1)
    before = latest((rel[:, None] == rel[None, :]) & (at[None, :] < at[:, None]))
    last = latest(rel[None, :] == jnp.arange(nrel, dtype=jnp.int32)[:, None])
    before, last = (jnp.where(found < 0, blocks, found) for found in (before, last))
    info = jnp.concatenate([rel, before, last])
    src = sources[0][:, None]
    tgt = targets[0][:, None]
    neg = negatives[0].reshape(-1, 1, negatives.shape[-1])
    L, LS, R, RS, partial, near = train_call(
        info, operators, left.T, left_state[None], right.T, right_state[None], src, tgt, neg, nrel
    )
    op_grad = final_share(reduce_call(partial, near), width)
    return (L.T, LS[0], R.T.astype(jnp.float32), RS[0], op_grad)


def solution(mesh):
    in_specs = (
        P(("blk", "rel"), None),
        P(("blk", "rel")),
        P(("blk", "rel"), None),
        P(("blk", "rel")),
        P("rel", None, None),
        P(("blk", "rel"), None, None),
        P(("blk", "rel"), None, None),
        P(("blk", "rel"), None, None),
        P(("blk", "rel"), None, None),
        P(("blk", "rel"), None, None, None),
    )
    out_specs = (
        P(("blk", "rel"), None),
        P(("blk", "rel")),
        P(("blk", "rel"), None),
        P(("blk", "rel")),
        P("rel", "blk"),
    )
    return jax.shard_map(body, mesh=mesh, in_specs=in_specs, out_specs=out_specs, check_vma=False)
```

```python
import functools
import jax
import jax.numpy as jnp
from jax import lax
from jax.experimental import pallas as pl
from jax.experimental.pallas import tpu as pltpu
from jax.sharding import PartitionSpec as P

BUCKETS = 3
STEP = 0.3
NT = (((1,), (1,)), ((), ()))
TN = (((0,), (0,)), ((), ()))
VMEM_LIMIT = 60 * 1024 * 1024
MESH = pl.DeviceIdType.MESH
UNITS = 4
LANES = 512
CHUNK = 512


def onehot(index, rows):
    index = index.astype(jnp.int16)
    row = lax.broadcasted_iota(jnp.int16, (rows, index.shape[1]), 0)
    one = jnp.ones((), jnp.bfloat16)
    return jnp.where(row == index, one, jnp.zeros((), jnp.bfloat16))


def dot(a, b, dims=None):
    if dims is None:
        return jnp.dot(a, b, preferred_element_type=jnp.float32)
    return lax.dot_general(a, b, dims, preferred_element_type=jnp.float32)


def place():
    b, r = lax.axis_index("blk"), lax.axis_index("rel")
    return b // 8, (b // 4) % 2, b % 4, r // 2, r % 2


def device(z, ylo, x, yhi, core):
    return (z * 8 + ylo * 4 + x, yhi * 2 + core)


def greet(peers):
    barrier = pltpu.get_barrier_semaphore()
    for peer in peers:
        pl.semaphore_signal(barrier, inc=1, device_id=peer, device_id_type=MESH)
    pl.semaphore_wait(barrier, len(peers))


def remote(src, dst, sems, index, peer):
    return pltpu.make_async_remote_copy(
        src_ref=src,
        dst_ref=dst,
        send_sem=sems[0].at[index],
        recv_sem=sems[1].at[index],
        device_id=peer,
        device_id_type=MESH,
    )


def send(src, dst, sems, index, peer):
    copy = remote(src, dst, sems, index, peer)
    copy.start()
    return copy


def adagrad(rows, acc, grad):
    acc = acc + jnp.sum(grad * grad, axis=0, keepdims=True) * (1.0 / grad.shape[0])
    return rows - STEP * grad * lax.rsqrt(acc), acc


def train_kernel(
    info_ref, own_ref, left_ref, lacc_ref, right_ref, racc_ref, src_ref, tgt_ref, neg_ref,
    newleft_ref, newlacc_ref, newright_ref, newracc_ref, grads_ref, near_ref,
    table, fresh_ref, freshacc_ref, half, rhalf, rhalf_t, hot, query, scaled, heads_now, push, scale, score, count, sums, rows_now, acc_now,
    in_rows, in_acc, load_sem, store_sem,
    cross_s, cross_r, ring_s, ring_r, whole_s, whole_r, pass_s, pass_r, move_s, move_r, acc_s, acc_r, near_s, near_r,
):
    z, ylo, x, yhi, core = place()
    me = yhi * 2 + core
    far = (1 - yhi) * 2 + core
    width, rows = newleft_ref.shape
    owned = own_ref.shape[0]
    units = owned * UNITS
    third = units // 8
    edges = src_ref.shape[2]
    nblk = (info_ref.shape[0] - table.shape[0]) // 2 // BUCKETS
    block = edges // nblk
    half_rows = rows // 2
    nrel = table.shape[0]
    total_blocks = BUCKETS * nblk
    blks = 32
    b, r = lax.axis_index("blk"), lax.axis_index("rel")
    ahead, behind = ((b + 1) % blks, r), ((b + blks - 1) % blks, r)
    sibling = device(z, ylo, x, yhi, 1 - core)
    cross = device(z, 1 - ylo, x, 1 - yhi, core)
    x_ring = [device(z, ylo, (x + d) % 4, yhi, core) for d in (1, 2, 3)]
    z_ring = [device((z + d) % 4, ylo, x, yhi, core) for d in (1, 2, 3)]
    loads = [
        pltpu.make_async_copy(left_ref, newleft_ref, load_sem.at[0]),
        pltpu.make_async_copy(right_ref, rows_now, load_sem.at[1]),
    ]
    for load in loads:
        load.start()
    greet([sibling, cross, ahead, behind] + x_ring + z_ring)

    for j in range(owned):
        table[me * owned + j] = jnp.pad(own_ref[j], ((0, 0), (0, LANES - width)))

    def unit(owner, u):
        lanes = LANES // UNITS
        return table.at[owner * owned + u // UNITS, :, pl.ds(pl.multiple_of((u % UNITS) * lanes, lanes), lanes)]

    first = [x * third, units // 2 + z * third]
    arrivals = {}
    for i in range(third):
        for ring in range(2):
            part = unit(me, first[ring] + i)
            arrivals[ring, i] = send(part, part, (cross_s, cross_r), ring * third + i, cross)
    mine = table.at[pl.ds(me * owned, owned)]
    copies = [send(mine, mine, (whole_s, whole_r), 0, sibling)]

    def heads(t):
        for c in range(0, edges, CHUNK):
            cols = slice(c, c + CHUNK)
            hot[:, cols] = onehot(src_ref[t, :, cols], rows)
            heads_now[:, cols] = dot(half[...], hot[:, cols]).astype(jnp.bfloat16)

    def counts(t):
        found = jnp.zeros((rows, 128), jnp.float32)
        for c in range(0, edges, CHUNK):
            of = (lax.broadcasted_iota(jnp.int32, (CHUNK, 128), 0) + c) // block
            share = jnp.where(of == lax.broadcasted_iota(jnp.int32, (CHUNK, 128), 1), 1.0 / block, 0.0)
            found += dot(onehot(neg_ref[t, :, c : c + CHUNK], rows), share.astype(jnp.bfloat16))
        count[t] = found

    def clear(n, carry):
        sums[n] = jnp.zeros(sums.shape[1:], jnp.float32)
        return carry

    newlacc_ref[...] = lacc_ref[...]
    acc_now[...] = racc_ref[...]
    for load in loads:
        load.wait()
    half[...] = newleft_ref[...].astype(jnp.bfloat16)
    heads(0)
    rings = (x_ring, z_ring)
    landed = {}
    for i in range(third):
        for ring in range(2):
            arrivals[ring, i].wait()
            part = unit(far, first[ring] + i)
            for d in (2, 1, 3):
                landed[ring, d, i] = send(
                    part, part, (ring_s, ring_r), (ring * 3 + d - 1) * third + i, rings[ring][d - 1]
                )
            copies.append(send(part, part, (pass_s, pass_r), ring * 4 * third + i, sibling))
        counts(i)
        if i == 1:
            lax.fori_loop(0, sums.shape[0], clear, 0)
    for i in range(third):
        for ring in range(2):
            for d in (1, 3, 2):
                landed[ring, d, i].wait()
                origin = ((x, z)[ring] - d + 4) % 4
                part = unit(far, ring * (units // 2) + origin * third + i)
                copies.append(send(part, part, (pass_s, pass_r), (ring * 4 + d) * third + i, sibling))
    for copy in copies:
        copy.wait()

    def operator(t, k):
        return table[info_ref[t * nblk + k]][:, :width]

    def earlier(n):
        return jnp.where(n < total_blocks, sums[jnp.minimum(n, total_blocks - 1)], 0.0)

    def moves(t, c, to_rows, to_acc):
        part = pl.ds(c * half_rows, half_rows)
        return (
            remote(fresh_ref.at[:, part], to_rows.at[:, part], (move_s, move_r), 2 * t + c, ahead),
            remote(freshacc_ref.at[:, part], to_acc.at[:, part], (acc_s, acc_r), 2 * t + c, ahead),
        )

    def queries(t):
        for k in range(nblk):
            cols = slice(k * block, (k + 1) * block)
            query[:, cols] = dot(operator(t, k), heads_now[:, cols], TN).astype(jnp.bfloat16)

    def start(copies):
        for copy in copies:
            copy.start()

    def bucket(t, carry):
        for c in range(2):
            part = slice(c * half_rows, (c + 1) * half_rows)

            @pl.when(t > 0)
            def _():
                for move in moves(t - 1, c, in_rows.at[t - 1], in_acc.at[t - 1]):
                    move.wait()
                rows_now[:, part] = in_rows[t - 1, :, part].astype(jnp.float32)
                acc_now[:, part] = in_acc[t - 1, :, part]

            rhalf[:, part] = rows_now[:, part].astype(jnp.bfloat16)
            rhalf_t[part, :] = rhalf[:, part].T

            def meet(j):
                cols = slice(j * CHUNK, (j + 1) * CHUNK)
                value = dot(rhalf_t[part, :], query[:, cols])
                score[j % 2] = value
                target = tgt_ref[t, :, cols] - c * half_rows
                hit = lax.broadcasted_iota(jnp.int32, (half_rows, CHUNK), 0) == target
                pos = jnp.sum(jnp.where(hit, value, 0.0), axis=0, keepdims=True)
                scale[c, :, cols] = jax.nn.sigmoid(-pos)

            def weigh(j):
                cols = slice(j * CHUNK, (j + 1) * CHUNK)
                target = tgt_ref[t, :, cols] - c * half_rows
                pull = scale[c, :, cols]
                size = jnp.where((target >= 0) & (target < half_rows), jnp.maximum(pull, 2.0**-8), 1.0)
                inverse = 1.0 / size
                times = [
                    jnp.broadcast_to(count[t, part, k : k + 1], (half_rows, block)).astype(jnp.bfloat16)
                    for k in range(j * CHUNK // block, (j + 1) * CHUNK // block)
                ]
                twice = (jnp.tanh(0.5 * score[j % 2]) + 1.0).astype(jnp.bfloat16)
                push[part, cols] = twice * (0.5 * inverse).astype(jnp.bfloat16) * jnp.concatenate(
                    times, axis=1
                ) - onehot(target, half_rows) * (pull * inverse).astype(jnp.bfloat16)
                scale[c, :, cols] = size
                scaled[:, cols] = (query[:, cols].astype(jnp.float32) * size).astype(jnp.bfloat16)

            meet(0)
            for j in range(1, edges // CHUNK):
                meet(j)
                weigh(j - 1)
            weigh(edges // CHUNK - 1)
            fresh, acc = adagrad(rows_now[:, part], acc_now[:, part], dot(scaled[...], push[part, :], NT))
            fresh_ref[:, part] = fresh.astype(jnp.bfloat16)
            freshacc_ref[:, part] = acc

            @pl.when(t < BUCKETS - 1)
            def _():
                start(moves(t, c, in_rows.at[t], in_acc.at[t]))

            @pl.when(t == BUCKETS - 1)
            def _():
                start(moves(BUCKETS - 1, c, newright_ref, newracc_ref))

        for j in range(0, edges, CHUNK):
            cols = slice(j, j + CHUNK)
            scaled[:, cols] = (
                dot(rhalf[:, :half_rows], push[:half_rows, cols]) * scale[0, :, cols]
                + dot(rhalf[:, half_rows:], push[half_rows:, cols]) * scale[1, :, cols]
            ).astype(jnp.bfloat16)
        for k in range(nblk):
            cols = slice(k * block, (k + 1) * block)
            query[:, cols] = dot(operator(t, k), scaled[:, cols]).astype(jnp.bfloat16)
        for c in range(0, rows, CHUNK):
            part = slice(c, c + CHUNK)
            left, acc = adagrad(newleft_ref[:, part], newlacc_ref[:, part], dot(query[...], hot[part, :], NT))
            newleft_ref[:, part] = left
            newlacc_ref[:, part] = acc
            half[:, part] = left.astype(jnp.bfloat16)
        for k in range(nblk):
            cols = slice(k * block, (k + 1) * block)
            before = earlier(info_ref[total_blocks + t * nblk + k])
            sums[t * nblk + k] = before + dot(heads_now[:, cols], scaled[:, cols], NT)

        @pl.when(t < BUCKETS - 1)
        def _():
            heads(t + 1)
            queries(t + 1)

        return carry

    queries(0)
    lax.fori_loop(0, BUCKETS, bucket, 0)

    copies = []
    for here in (False, True):
        for n in range(nrel // 2):
            part, h, i = n // 4, n // 2 % 2, n % 2
            j = (h * 2 + (core if here else 1 - core)) * owned + part * 2 + i
            table[j, :, :width] = earlier(info_ref[2 * total_blocks + j]).astype(jnp.bfloat16)
            if here:
                copy = pltpu.make_async_copy(table.at[j], grads_ref.at[part, h * 2 + i], store_sem.at[n])
                copy.start()
            else:
                copy = send(table.at[j], near_ref.at[part, h * 2 + i], (near_s, near_r), n, sibling)
            copies.append(copy)
    for copy in copies:
        copy.wait()
    for c in range(2):
        for move in moves(BUCKETS - 1, c, newright_ref, newracc_ref):
            move.wait()


def train_call(info, own, left, lacc, right, racc, src, tgt, neg, nrel, nblk):
    width, rows = left.shape
    owned = own.shape[0]
    units = owned * UNITS
    third = units // 8
    buckets, _, edges = src.shape
    dma = lambda n: [pltpu.SemaphoreType.DMA((n,))] * 2
    vmem = pl.BlockSpec(memory_space=pltpu.VMEM)
    anywhere = pl.BlockSpec(memory_space=pl.ANY)
    f32, bf16 = jnp.float32, jnp.bfloat16
    return pl.pallas_call(
        train_kernel,
        in_specs=[pl.BlockSpec(memory_space=pltpu.SMEM), vmem, anywhere, vmem, anywhere] + [vmem] * 4,
        out_specs=[vmem] * 2 + [anywhere] * 4,
        out_shape=[
            jax.ShapeDtypeStruct((width, rows), f32),
            jax.ShapeDtypeStruct((1, rows), f32),
            jax.ShapeDtypeStruct((width, rows), bf16),
            jax.ShapeDtypeStruct((1, rows), f32),
            jax.ShapeDtypeStruct((3, nrel // 6, width, LANES), bf16),
            jax.ShapeDtypeStruct((3, nrel // 6, width, LANES), bf16),
        ],
        scratch_shapes=[
            pltpu.VMEM((nrel, width, LANES), bf16),
            pltpu.VMEM((width, rows), bf16),
            pltpu.VMEM((1, rows), f32),
            pltpu.VMEM((width, rows), bf16),
            pltpu.VMEM((width, rows), bf16),
            pltpu.VMEM((rows, width), bf16),
            pltpu.VMEM((rows, edges), bf16),
            pltpu.VMEM((width, edges), bf16),
            pltpu.VMEM((width, edges), bf16),
            pltpu.VMEM((width, edges), bf16),
            pltpu.VMEM((rows, edges), bf16),
            pltpu.VMEM((2, 1, edges), f32),
            pltpu.VMEM((2, rows // 2, CHUNK), f32),
            pltpu.VMEM((buckets, rows, 128), f32),
            pltpu.VMEM((buckets * nblk, width, width), f32),
            pltpu.VMEM((width, rows), f32),
            pltpu.VMEM((1, rows), f32),
            pltpu.VMEM((buckets - 1, width, rows), bf16),
            pltpu.VMEM((buckets - 1, 1, rows), f32),
            pltpu.SemaphoreType.DMA((2,)),
            pltpu.SemaphoreType.DMA((nrel // 2,)),
        ]
        + dma(2 * third) + dma(6 * third) + dma(1) + dma(8 * third) + dma(2 * buckets) + dma(2 * buckets) + dma(nrel // 2),
        compiler_params=pltpu.CompilerParams(
            collective_id=0, has_side_effects=True, vmem_limit_bytes=VMEM_LIMIT
        ),
        name="train_buckets",
    )(info, own, left, lacc, right, racc, src, tgt, neg)


def row_of(t):
    return 25 * t // 2


def last_window(s, t):
    if s == 0:
        base, top = 96 * (t // 8) + 48 * ((t // 4) % 2), 48
    elif s == 1:
        base, top = 192 * (t // 16) + 48 * ((t // 4) % 4), 48
    else:
        z = (t // 2) % 4
        base, top = 96 * (t // 8) + 16 * z + 16 * (z // 2), 32
    part = row_of(t) - base
    local = 16 * (part // 16) - 16 * (part // top)
    return base + local, local


def window(start, size):
    return pl.ds(pl.multiple_of(start, 16), size)


def total(out, own, parts):
    value = own.astype(jnp.float32)
    for part in parts:
        value = value + part.astype(jnp.float32)
    out[...] = value.astype(out.dtype)


def reduce_kernel(
    grads_ref, near_ref, out_ref, own, near,
    a0, b0, c0, a1, b1, c1, a2, b2, c2, m0, n0, m1, n1, m2, n2, own_sem, near_sem, send_sem, recv_sem,
):
    z, ylo, x, yhi, core = place()
    sems = (send_sem, recv_sem)
    z_at = [(z + d) % 4 for d in (1, 2, 3)]
    x_at = [(x + d) % 4 for d in (1, 2, 3)]
    y_at = [(yhi, 1 - ylo), (1 - yhi, ylo), (1 - yhi, 1 - ylo)]
    z_ring = [device(v, ylo, x, yhi, core) for v in z_at]
    x_ring = [device(z, ylo, v, yhi, core) for v in x_at]
    y_ring = [device(z, v, x, h, core) for h, v in y_at]
    mine, pairs = [], []
    for s in range(3):
        pairs.append(pltpu.make_async_copy(near_ref.at[s], near.at[s], near_sem.at[s]))
        mine.append(pltpu.make_async_copy(grads_ref.at[s], own.at[s], own_sem.at[s]))
        pairs[-1].start()
        mine[-1].start()
    greet(z_ring + x_ring + y_ring)

    first = []
    for s in range(3):
        mine[s].wait()
        pairs[s].wait()
        for i in range(4):
            total(own.at[s, i], own[s, i], [near[s, i]])
        for d in range(3):
            if s == 0:
                src = own.at[s, :, window(96 * z_at[d], 112)]
                copy = send(src, a0.at[d], sems, 3 + s * 3 + d, z_ring[d])
            elif s == 1:
                h, v = y_at[d]
                src = own.at[s, pl.ds(2 * h, 2), window(192 * v, 208)]
                copy = send(src, a1.at[d], sems, 3 + s * 3 + d, y_ring[d])
            else:
                src = own.at[s, :, window(96 * x_at[d], 112)]
                copy = send(src, a2.at[d], sems, 3 + s * 3 + d, x_ring[d])
            first.append(copy)

    second = []
    for s in range(3):
        for d in range(3):
            first[s * 3 + d].wait()
        if s == 0:
            total(m0, own[s, :, window(96 * z, 112)], [a0[d] for d in range(3)])
        elif s == 1:
            total(m1, own[s, pl.ds(2 * yhi, 2), window(192 * ylo, 208)], [a1[d] for d in range(3)])
        else:
            total(m2, own[s, :, window(96 * x, 112)], [a2[d] for d in range(3)])
        for d in range(3):
            if s == 0:
                h, v = y_at[d]
                copy = send(m0.at[pl.ds(2 * h, 2), window(48 * v, 64)], b0.at[d], sems, 12 + s * 3 + d, y_ring[d])
            elif s == 1:
                copy = send(m1.at[:, window(48 * x_at[d], 64)], b1.at[d], sems, 12 + s * 3 + d, x_ring[d])
            else:
                v = z_at[d]
                copy = send(m2.at[:, window(16 * v + 16 * (v // 2), 48)], b2.at[d], sems, 12 + s * 3 + d, z_ring[d])
            second.append(copy)

    third = []
    for s in range(3):
        for d in range(3):
            second[s * 3 + d].wait()
        if s == 0:
            total(n0, m0[pl.ds(2 * yhi, 2), window(48 * ylo, 64)], [b0[d] for d in range(3)])
        elif s == 1:
            total(n1, m1[:, window(48 * x, 64)], [b1[d] for d in range(3)])
        else:
            total(n2, m2[:, window(16 * z + 16 * (z // 2), 48)], [b2[d] for d in range(3)])
        for d in range(3):
            if s == 0:
                _, at = last_window(0, z * 8 + ylo * 4 + x_at[d])
                copy = send(n0.at[:, window(at, 32)], c0.at[d], sems, 21 + s * 3 + d, x_ring[d])
            elif s == 1:
                _, at = last_window(1, ylo * 16 + x * 4 + z_at[d])
                copy = send(n1.at[:, window(at, 32)], c1.at[d], sems, 21 + s * 3 + d, z_ring[d])
            else:
                h, v = y_at[d]
                _, at = last_window(2, x * 8 + z * 2 + v)
                copy = send(n2.at[pl.ds(2 * h, 2), window(at, 32)], c2.at[d], sems, 21 + s * 3 + d, y_ring[d])
            third.append(copy)

    for s in range(3):
        for d in range(3):
            third[s * 3 + d].wait()
        if s == 0:
            _, at = last_window(0, z * 8 + ylo * 4 + x)
            total(out_ref.at[s], n0[:, window(at, 32)], [c0[d] for d in range(3)])
        elif s == 1:
            _, at = last_window(1, ylo * 16 + x * 4 + z)
            total(out_ref.at[s], n1[:, window(at, 32)], [c1[d] for d in range(3)])
        else:
            _, at = last_window(2, x * 8 + z * 2 + ylo)
            total(out_ref.at[s], n2[pl.ds(2 * yhi, 2), window(at, 32)], [c2[d] for d in range(3)])


def reduce_call(grads, near):
    _, four, rows, lanes = grads.shape
    buf = lambda *shape: pltpu.VMEM(shape + (lanes,), jnp.bfloat16)
    return pl.pallas_call(
        reduce_kernel,
        in_specs=[pl.BlockSpec(memory_space=pl.ANY)] * 2,
        out_specs=pl.BlockSpec(memory_space=pltpu.VMEM),
        out_shape=jax.ShapeDtypeStruct((3, 2, 32, lanes), jnp.float32),
        scratch_shapes=[
            buf(3, four, rows), buf(3, four, rows),
            buf(3, 4, 112), buf(3, 2, 64), buf(3, 2, 32),
            buf(3, 2, 208), buf(3, 2, 64), buf(3, 2, 32),
            buf(3, 4, 112), buf(3, 4, 48), buf(3, 2, 32),
            buf(4, 112), buf(2, 64), buf(2, 208), buf(2, 64), buf(4, 112), buf(4, 48),
            pltpu.SemaphoreType.DMA((3,)), pltpu.SemaphoreType.DMA((3,)), pltpu.SemaphoreType.DMA((30,)), pltpu.SemaphoreType.DMA((30,)),
        ],
        compiler_params=pltpu.CompilerParams(
            collective_id=1, has_side_effects=True, vmem_limit_bytes=VMEM_LIMIT
        ),
        name="reduce_operator_gradients",
    )(grads, near)


def final_share(pieces, width):
    blk = lax.axis_size("blk")
    place_1 = lambda b: ((b // 4) % 2) * 16 + (b % 4) * 4 + b // 8
    place_2 = lambda b: (b % 4) * 8 + (b // 8) * 2 + (b // 4) % 2
    t = lax.axis_index("blk")
    shares = []
    for s, at in enumerate((None, place_1, place_2)):
        piece = pieces[s, :, :, :width]
        if at is not None:
            piece = lax.ppermute(piece, "blk", [(b, at(b)) for b in range(blk)])
        start, _ = last_window(s, t)
        skip = t * (width * width // blk) - start * width
        flat = piece.reshape(2, 32 * width)
        shares.append(lax.dynamic_slice(flat, (0, skip), (2, width * width // blk)))
    return jnp.concatenate(shares, axis=0)


def body(left, left_state, right, right_state, operators, need_list, block_slot, sources, targets, negatives):
    owned_count, width, _ = operators.shape
    owners = lax.axis_size("rel")
    nrel = owned_count * owners
    rel = need_list[0].reshape(-1)[block_slot[0].reshape(-1)]
    blocks = rel.shape[0]
    at = jnp.arange(blocks, dtype=jnp.int32)
    latest = lambda found: jnp.max(jnp.where(found, at, -1), axis=1)
    before = latest((rel[:, None] == rel[None, :]) & (at[None, :] < at[:, None]))
    last = latest(rel[None, :] == jnp.arange(nrel, dtype=jnp.int32)[:, None])
    before, last = (jnp.where(found < 0, blocks, found) for found in (before, last))
    info = jnp.concatenate([rel, before, last])
    src = sources[0][:, None]
    tgt = targets[0][:, None]
    neg = negatives[0].reshape(BUCKETS, 1, -1)
    L, LS, R, RS, partial, near = train_call(
        info, operators, left.T, left_state[None], right.T, right_state[None], src, tgt, neg, nrel, block_slot.shape[-1]
    )
    op_grad = final_share(reduce_call(partial, near), width)
    return (L.T, LS[0], R.T.astype(jnp.float32), RS[0], op_grad)


def solution(mesh):
    in_specs = (
        P(("blk", "rel"), None),
        P(("blk", "rel")),
        P(("blk", "rel"), None),
        P(("blk", "rel")),
        P("rel", None, None),
        P(("blk", "rel"), None, None),
        P(("blk", "rel"), None, None),
        P(("blk", "rel"), None, None),
        P(("blk", "rel"), None, None),
        P(("blk", "rel"), None, None, None),
    )
    out_specs = (
        P(("blk", "rel"), None),
        P(("blk", "rel")),
        P(("blk", "rel"), None),
        P(("blk", "rel")),
        P("rel", "blk"),
    )
    return jax.shard_map(body, mesh=mesh, in_specs=in_specs, out_specs=out_specs, check_vma=False)
```

```python
import functools
import jax
import jax.numpy as jnp
from jax import lax
from jax.experimental import pallas as pl
from jax.experimental.pallas import tpu as pltpu
from jax.sharding import PartitionSpec as P

BUCKETS = 3
STEP = 0.3
NT = (((1,), (1,)), ((), ()))
TN = (((0,), (0,)), ((), ()))
VMEM_LIMIT = 60 * 1024 * 1024
MESH = pl.DeviceIdType.MESH
UNITS = 4
LANES = 512
CHUNK = 512


def onehot(index, rows):
    index = index.astype(jnp.int16)
    row = lax.broadcasted_iota(jnp.int16, (rows, index.shape[1]), 0)
    one = jnp.ones((), jnp.bfloat16)
    return jnp.where(row == index, one, jnp.zeros((), jnp.bfloat16))


def dot(a, b, dims=None):
    if dims is None:
        return jnp.dot(a, b, preferred_element_type=jnp.float32)
    return lax.dot_general(a, b, dims, preferred_element_type=jnp.float32)


def place():
    b, r = lax.axis_index("blk"), lax.axis_index("rel")
    return b // 8, (b // 4) % 2, b % 4, r // 2, r % 2


def device(z, ylo, x, yhi, core):
    return (z * 8 + ylo * 4 + x, yhi * 2 + core)


def greet(peers):
    barrier = pltpu.get_barrier_semaphore()
    for peer in peers:
        pl.semaphore_signal(barrier, inc=1, device_id=peer, device_id_type=MESH)
    pl.semaphore_wait(barrier, len(peers))


def remote(src, dst, sems, index, peer):
    return pltpu.make_async_remote_copy(
        src_ref=src,
        dst_ref=dst,
        send_sem=sems[0].at[index],
        recv_sem=sems[1].at[index],
        device_id=peer,
        device_id_type=MESH,
    )


def send(src, dst, sems, index, peer):
    copy = remote(src, dst, sems, index, peer)
    copy.start()
    return copy


def adagrad(rows, acc, grad):
    acc = acc + jnp.sum(grad * grad, axis=0, keepdims=True) * (1.0 / grad.shape[0])
    return rows - STEP * grad * lax.rsqrt(acc), acc


def row_of(t):
    return 25 * t // 2


def last_window(s, t):
    if s == 0:
        base, top = 96 * (t // 8) + 48 * ((t // 4) % 2), 48
    elif s == 1:
        base, top = 192 * (t // 16) + 48 * ((t // 4) % 4), 48
    else:
        z = (t // 2) % 4
        base, top = 96 * (t // 8) + 16 * z + 16 * (z // 2), 32
    part = row_of(t) - base
    local = 16 * (part // 16) - 16 * (part // top)
    return base + local, local


def window(start, size):
    return pl.ds(pl.multiple_of(start, 16), size)


def total(out, own, parts):
    value = own.astype(jnp.float32)
    for part in parts:
        value = value + part.astype(jnp.float32)
    out[...] = value.astype(out.dtype)


def train_kernel(
    info_ref, own_ref, left_ref, lacc_ref, right_ref, racc_ref, src_ref, tgt_ref, neg_ref,
    newleft_ref, newlacc_ref, newright_ref, newracc_ref, out_ref,
    table, fresh_ref, freshacc_ref, half, rhalf, rhalf_t, hot, query, scaled, heads_now, push, scale, score, count, sums, rows_now, acc_now,
    in_rows, in_acc, near, a0, b0, c0, a1, b1, c1, a2, b2, c2, load_sem,
    cross_s, cross_r, ring_s, ring_r, whole_s, whole_r, pass_s, pass_r, move_s, move_r, acc_s, acc_r, near_s, near_r, sum_s, sum_r,
):
    z, ylo, x, yhi, core = place()
    me = yhi * 2 + core
    far = (1 - yhi) * 2 + core
    width, rows = newleft_ref.shape
    owned = own_ref.shape[0]
    units = owned * UNITS
    third = units // 8
    edges = src_ref.shape[2]
    nblk = (info_ref.shape[0] - table.shape[0]) // 2 // BUCKETS
    block = edges // nblk
    half_rows = rows // 2
    nrel = table.shape[0]
    total_blocks = BUCKETS * nblk
    blks = 32
    b, r = lax.axis_index("blk"), lax.axis_index("rel")
    ahead, behind = ((b + 1) % blks, r), ((b + blks - 1) % blks, r)
    sibling = device(z, ylo, x, yhi, 1 - core)
    cross = device(z, 1 - ylo, x, 1 - yhi, core)
    x_ring = [device(z, ylo, (x + d) % 4, yhi, core) for d in (1, 2, 3)]
    z_ring = [device((z + d) % 4, ylo, x, yhi, core) for d in (1, 2, 3)]
    loads = [
        pltpu.make_async_copy(left_ref, newleft_ref, load_sem.at[0]),
        pltpu.make_async_copy(right_ref, rows_now, load_sem.at[1]),
    ]
    for load in loads:
        load.start()
    x_at = [(x + d) % 4 for d in (1, 2, 3)]
    z_at = [(z + d) % 4 for d in (1, 2, 3)]
    y_at = [(yhi, 1 - ylo), (1 - yhi, ylo), (1 - yhi, 1 - ylo)]
    y_ring = [device(z, v, x, h, core) for h, v in y_at]
    greet([sibling, ahead, behind] + x_ring + y_ring + z_ring)

    for j in range(owned):
        table[me * owned + j] = jnp.pad(own_ref[j], ((0, 0), (0, LANES - width)))

    def unit(owner, u):
        lanes = LANES // UNITS
        return table.at[owner * owned + u // UNITS, :, pl.ds(pl.multiple_of((u % UNITS) * lanes, lanes), lanes)]

    first = [x * third, units // 2 + z * third]
    arrivals = {}
    for i in range(third):
        for ring in range(2):
            part = unit(me, first[ring] + i)
            arrivals[ring, i] = send(part, part, (cross_s, cross_r), ring * third + i, cross)
    mine = table.at[pl.ds(me * owned, owned)]
    copies = [send(mine, mine, (whole_s, whole_r), 0, sibling)]

    def heads(t):
        for c in range(0, edges, CHUNK):
            cols = slice(c, c + CHUNK)
            hot[:, cols] = onehot(src_ref[t, :, cols], rows)
            heads_now[:, cols] = dot(half[...], hot[:, cols]).astype(jnp.bfloat16)

    def counts(t):
        found = jnp.zeros((rows, 128), jnp.float32)
        for c in range(0, edges, CHUNK):
            of = (lax.broadcasted_iota(jnp.int32, (CHUNK, 128), 0) + c) // block
            share = jnp.where(of == lax.broadcasted_iota(jnp.int32, (CHUNK, 128), 1), 1.0 / block, 0.0)
            found += dot(onehot(neg_ref[t, :, c : c + CHUNK], rows), share.astype(jnp.bfloat16))
        count[t] = found

    def clear(n, carry):
        sums[n] = jnp.zeros(sums.shape[1:], sums.dtype)
        return carry

    newlacc_ref[...] = lacc_ref[...]
    acc_now[...] = racc_ref[...]
    for load in loads:
        load.wait()
    half[...] = newleft_ref[...].astype(jnp.bfloat16)
    heads(0)
    rings = (x_ring, z_ring)
    landed = {}
    for i in range(third):
        for ring in range(2):
            arrivals[ring, i].wait()
            part = unit(far, first[ring] + i)
            for d in (2, 1, 3):
                landed[ring, d, i] = send(
                    part, part, (ring_s, ring_r), (ring * 3 + d - 1) * third + i, rings[ring][d - 1]
                )
            copies.append(send(part, part, (pass_s, pass_r), ring * 4 * third + i, sibling))
        counts(i)
        if i == 1:
            lax.fori_loop(0, sums.shape[0], clear, 0)
    for i in range(third):
        for ring in range(2):
            for d in (1, 3, 2):
                landed[ring, d, i].wait()
                origin = ((x, z)[ring] - d + 4) % 4
                part = unit(far, ring * (units // 2) + origin * third + i)
                copies.append(send(part, part, (pass_s, pass_r), (ring * 4 + d) * third + i, sibling))
    for copy in copies:
        copy.wait()

    def operator(t, k):
        return table[info_ref[t * nblk + k]][:, :width]

    def earlier(n):
        return jnp.where(n < total_blocks, sums[jnp.minimum(n, total_blocks - 1)].astype(jnp.float32), 0.0)

    def moves(t, c, to_rows, to_acc):
        part = pl.ds(c * half_rows, half_rows)
        return (
            remote(fresh_ref.at[:, part], to_rows.at[:, part], (move_s, move_r), 2 * t + c, ahead),
            remote(freshacc_ref.at[:, part], to_acc.at[:, part], (acc_s, acc_r), 2 * t + c, ahead),
        )

    def queries(t):
        for k in range(nblk):
            cols = slice(k * block, (k + 1) * block)
            query[:, cols] = dot(operator(t, k), heads_now[:, cols], TN).astype(jnp.bfloat16)

    def start(copies):
        for copy in copies:
            copy.start()

    def bucket(t, carry):
        for c in range(2):
            part = slice(c * half_rows, (c + 1) * half_rows)

            @pl.when(t > 0)
            def _():
                for move in moves(t - 1, c, in_rows.at[t - 1], in_acc.at[t - 1]):
                    move.wait()
                rows_now[:, part] = in_rows[t - 1, :, part].astype(jnp.float32)
                acc_now[:, part] = in_acc[t - 1, :, part]

            rhalf[:, part] = rows_now[:, part].astype(jnp.bfloat16)
            rhalf_t[part, :] = rhalf[:, part].T

            def meet(j):
                cols = slice(j * CHUNK, (j + 1) * CHUNK)
                value = dot(rhalf_t[part, :], query[:, cols])
                score[j % 2] = value
                target = tgt_ref[t, :, cols] - c * half_rows
                hit = lax.broadcasted_iota(jnp.int32, (half_rows, CHUNK), 0) == target
                pos = jnp.sum(jnp.where(hit, value, 0.0), axis=0, keepdims=True)
                scale[c, :, cols] = jax.nn.sigmoid(-pos)

            def weigh(j):
                cols = slice(j * CHUNK, (j + 1) * CHUNK)
                target = tgt_ref[t, :, cols] - c * half_rows
                pull = scale[c, :, cols]
                size = jnp.where((target >= 0) & (target < half_rows), jnp.maximum(pull, 2.0**-8), 1.0)
                inverse = 1.0 / size
                times = [
                    jnp.broadcast_to(count[t, part, k : k + 1], (half_rows, block)).astype(jnp.bfloat16)
                    for k in range(j * CHUNK // block, (j + 1) * CHUNK // block)
                ]
                twice = (jnp.tanh(0.5 * score[j % 2]) + 1.0).astype(jnp.bfloat16)
                push[part, cols] = twice * (0.5 * inverse).astype(jnp.bfloat16) * jnp.concatenate(
                    times, axis=1
                ) - onehot(target, half_rows) * (pull * inverse).astype(jnp.bfloat16)
                scale[c, :, cols] = size
                scaled[:, cols] = (query[:, cols].astype(jnp.float32) * size).astype(jnp.bfloat16)

            meet(0)
            for j in range(1, edges // CHUNK):
                meet(j)
                weigh(j - 1)
            weigh(edges // CHUNK - 1)
            fresh, acc = adagrad(rows_now[:, part], acc_now[:, part], dot(scaled[...], push[part, :], NT))
            fresh_ref[:, part] = fresh.astype(jnp.bfloat16)
            freshacc_ref[:, part] = acc

            @pl.when(t < BUCKETS - 1)
            def _():
                start(moves(t, c, in_rows.at[t], in_acc.at[t]))

            @pl.when(t == BUCKETS - 1)
            def _():
                start(moves(BUCKETS - 1, c, newright_ref, newracc_ref))

        for j in range(0, edges, CHUNK):
            cols = slice(j, j + CHUNK)
            scaled[:, cols] = (
                dot(rhalf[:, :half_rows], push[:half_rows, cols]) * scale[0, :, cols]
                + dot(rhalf[:, half_rows:], push[half_rows:, cols]) * scale[1, :, cols]
            ).astype(jnp.bfloat16)
        for k in range(nblk):
            cols = slice(k * block, (k + 1) * block)
            query[:, cols] = dot(operator(t, k), scaled[:, cols]).astype(jnp.bfloat16)
        for c in range(0, rows, CHUNK):
            part = slice(c, c + CHUNK)
            left, acc = adagrad(newleft_ref[:, part], newlacc_ref[:, part], dot(query[...], hot[part, :], NT))
            newleft_ref[:, part] = left
            newlacc_ref[:, part] = acc
            half[:, part] = left.astype(jnp.bfloat16)
        for k in range(nblk):
            cols = slice(k * block, (k + 1) * block)
            before = earlier(info_ref[total_blocks + t * nblk + k])
            sums[t * nblk + k] = (before + dot(heads_now[:, cols], scaled[:, cols], NT)).astype(sums.dtype)

        @pl.when(t < BUCKETS - 1)
        def _():
            heads(t + 1)
            queries(t + 1)

        return carry

    queries(0)
    lax.fori_loop(0, BUCKETS, bucket, 0)

    quarter = nrel // 6
    half_count = nrel // 2

    def relation(n, of_core):
        part, h, i = n // quarter, n // 2 % 2, n % 2
        return earlier(info_ref[2 * total_blocks + (h * 2 + of_core) * owned + part * 2 + i])

    pairs = []
    for n in range(half_count):
        table[half_count + n, :, :width] = relation(n, 1 - core).astype(jnp.bfloat16)
        pairs.append(send(table.at[half_count + n], near.at[n], (near_s, near_r), n, sibling))

    sems = (sum_s, sum_r)
    own = [table.at[pl.ds(s * quarter, quarter)] for s in range(3)]
    first = []
    for s in range(3):
        for n in range(s * quarter, (s + 1) * quarter):
            pairs[n].wait()
            table[n, :, :width] = (relation(n, core) + near[n, :, :width].astype(jnp.float32)).astype(jnp.bfloat16)
        for d in range(3):
            if s == 0:
                copy = send(own[s].at[:, window(96 * z_at[d], 112)], a0.at[d], sems, s * 3 + d, z_ring[d])
            elif s == 1:
                h, v = y_at[d]
                copy = send(own[s].at[pl.ds(2 * h, 2), window(192 * v, 208)], a1.at[d], sems, s * 3 + d, y_ring[d])
            else:
                copy = send(own[s].at[:, window(96 * x_at[d], 112)], a2.at[d], sems, s * 3 + d, x_ring[d])
            first.append(copy)

    second = []
    for s in range(3):
        for d in range(3):
            first[s * 3 + d].wait()
        if s == 0:
            total(a0.at[0], own[s][:, window(96 * z, 112)], [a0[d] for d in range(3)])
        elif s == 1:
            total(a1.at[0], own[s][pl.ds(2 * yhi, 2), window(192 * ylo, 208)], [a1[d] for d in range(3)])
        else:
            total(a2.at[0], own[s][:, window(96 * x, 112)], [a2[d] for d in range(3)])
        for d in range(3):
            if s == 0:
                h, v = y_at[d]
                src = a0.at[0, pl.ds(2 * h, 2), window(48 * v, 64)]
                copy = send(src, b0.at[d], sems, 9 + s * 3 + d, y_ring[d])
            elif s == 1:
                copy = send(a1.at[0, :, window(48 * x_at[d], 64)], b1.at[d], sems, 9 + s * 3 + d, x_ring[d])
            else:
                v = z_at[d]
                src = a2.at[0, :, window(16 * v + 16 * (v // 2), 48)]
                copy = send(src, b2.at[d], sems, 9 + s * 3 + d, z_ring[d])
            second.append(copy)

    third = []
    for s in range(3):
        for d in range(3):
            second[s * 3 + d].wait()
        if s == 0:
            total(b0.at[0], a0[0, pl.ds(2 * yhi, 2), window(48 * ylo, 64)], [b0[d] for d in range(3)])
        elif s == 1:
            total(b1.at[0], a1[0, :, window(48 * x, 64)], [b1[d] for d in range(3)])
        else:
            total(b2.at[0], a2[0, :, window(16 * z + 16 * (z // 2), 48)], [b2[d] for d in range(3)])
        for d in range(3):
            if s == 0:
                _, at = last_window(0, z * 8 + ylo * 4 + x_at[d])
                copy = send(b0.at[0, :, window(at, 32)], c0.at[d], sems, 18 + s * 3 + d, x_ring[d])
            elif s == 1:
                _, at = last_window(1, ylo * 16 + x * 4 + z_at[d])
                copy = send(b1.at[0, :, window(at, 32)], c1.at[d], sems, 18 + s * 3 + d, z_ring[d])
            else:
                h, v = y_at[d]
                _, at = last_window(2, x * 8 + z * 2 + v)
                src = b2.at[0, pl.ds(2 * h, 2), window(at, 32)]
                copy = send(src, c2.at[d], sems, 18 + s * 3 + d, y_ring[d])
            third.append(copy)

    for s in range(3):
        for d in range(3):
            third[s * 3 + d].wait()
        if s == 0:
            _, at = last_window(0, z * 8 + ylo * 4 + x)
            total(out_ref.at[s], b0[0, :, window(at, 32)], [c0[d] for d in range(3)])
        elif s == 1:
            _, at = last_window(1, ylo * 16 + x * 4 + z)
            total(out_ref.at[s], b1[0, :, window(at, 32)], [c1[d] for d in range(3)])
        else:
            _, at = last_window(2, x * 8 + z * 2 + ylo)
            total(out_ref.at[s], b2[0, pl.ds(2 * yhi, 2), window(at, 32)], [c2[d] for d in range(3)])

    for c in range(2):
        for move in moves(BUCKETS - 1, c, newright_ref, newracc_ref):
            move.wait()


def train_call(info, own, left, lacc, right, racc, src, tgt, neg, nrel, nblk):
    width, rows = left.shape
    owned = own.shape[0]
    units = owned * UNITS
    third = units // 8
    buckets, _, edges = src.shape
    dma = lambda n: [pltpu.SemaphoreType.DMA((n,))] * 2
    vmem = pl.BlockSpec(memory_space=pltpu.VMEM)
    anywhere = pl.BlockSpec(memory_space=pl.ANY)
    f32, bf16 = jnp.float32, jnp.bfloat16
    four = nrel // 6
    buf = lambda *shape: pltpu.VMEM(shape + (LANES,), bf16)
    return pl.pallas_call(
        train_kernel,
        in_specs=[pl.BlockSpec(memory_space=pltpu.SMEM), vmem, anywhere, vmem, anywhere] + [vmem] * 4,
        out_specs=[vmem] * 2 + [anywhere] * 2 + [vmem],
        out_shape=[
            jax.ShapeDtypeStruct((width, rows), f32),
            jax.ShapeDtypeStruct((1, rows), f32),
            jax.ShapeDtypeStruct((width, rows), bf16),
            jax.ShapeDtypeStruct((1, rows), f32),
            jax.ShapeDtypeStruct((3, 2, 32, LANES), f32),
        ],
        scratch_shapes=[
            pltpu.VMEM((nrel, width, LANES), bf16),
            pltpu.VMEM((width, rows), bf16),
            pltpu.VMEM((1, rows), f32),
            pltpu.VMEM((width, rows), bf16),
            pltpu.VMEM((width, rows), bf16),
            pltpu.VMEM((rows, width), bf16),
            pltpu.VMEM((rows, edges), bf16),
            pltpu.VMEM((width, edges), bf16),
            pltpu.VMEM((width, edges), bf16),
            pltpu.VMEM((width, edges), bf16),
            pltpu.VMEM((rows, edges), bf16),
            pltpu.VMEM((2, 1, edges), f32),
            pltpu.VMEM((2, rows // 2, CHUNK), f32),
            pltpu.VMEM((buckets, rows, 128), f32),
            pltpu.VMEM((buckets * nblk, width, width), bf16),
            pltpu.VMEM((width, rows), f32),
            pltpu.VMEM((1, rows), f32),
            pltpu.VMEM((buckets - 1, width, rows), bf16),
            pltpu.VMEM((buckets - 1, 1, rows), f32),
            pltpu.VMEM((nrel // 2, width, LANES), bf16),
            buf(3, four, 112), buf(3, 2, 64), buf(3, 2, 32),
            buf(3, 2, 208), buf(3, 2, 64), buf(3, 2, 32),
            buf(3, four, 112), buf(3, four, 48), buf(3, 2, 32),
            pltpu.SemaphoreType.DMA((2,)),
        ]
        + dma(2 * third) + dma(6 * third) + dma(1) + dma(8 * third) + dma(2 * buckets) + dma(2 * buckets) + dma(nrel // 2) + dma(27),
        compiler_params=pltpu.CompilerParams(
            collective_id=0, has_side_effects=True, vmem_limit_bytes=VMEM_LIMIT
        ),
        name="train_buckets",
    )(info, own, left, lacc, right, racc, src, tgt, neg)


def final_share(pieces, width):
    blk = lax.axis_size("blk")
    place_1 = lambda b: ((b // 4) % 2) * 16 + (b % 4) * 4 + b // 8
    place_2 = lambda b: (b % 4) * 8 + (b // 8) * 2 + (b // 4) % 2
    t = lax.axis_index("blk")
    shares = []
    for s, at in enumerate((None, place_1, place_2)):
        piece = pieces[s, :, :, :width]
        if at is not None:
            piece = lax.ppermute(piece, "blk", [(b, at(b)) for b in range(blk)])
        start, _ = last_window(s, t)
        skip = t * (width * width // blk) - start * width
        flat = piece.reshape(2, 32 * width)
        shares.append(lax.dynamic_slice(flat, (0, skip), (2, width * width // blk)))
    return jnp.concatenate(shares, axis=0)


def body(left, left_state, right, right_state, operators, need_list, block_slot, sources, targets, negatives):
    owned_count, width, _ = operators.shape
    owners = lax.axis_size("rel")
    nrel = owned_count * owners
    rel = need_list[0].reshape(-1)[block_slot[0].reshape(-1)]
    blocks = rel.shape[0]
    at = jnp.arange(blocks, dtype=jnp.int32)
    latest = lambda found: jnp.max(jnp.where(found, at, -1), axis=1)
    before = latest((rel[:, None] == rel[None, :]) & (at[None, :] < at[:, None]))
    last = latest(rel[None, :] == jnp.arange(nrel, dtype=jnp.int32)[:, None])
    before, last = (jnp.where(found < 0, blocks, found) for found in (before, last))
    info = jnp.concatenate([rel, before, last])
    src = sources[0][:, None]
    tgt = targets[0][:, None]
    neg = negatives[0].reshape(BUCKETS, 1, -1)
    L, LS, R, RS, pieces = train_call(
        info, operators, left.T, left_state[None], right.T, right_state[None], src, tgt, neg, nrel, block_slot.shape[-1]
    )
    op_grad = final_share(pieces, width)
    return (L.T, LS[0], R.T.astype(jnp.float32), RS[0], op_grad)


def solution(mesh):
    in_specs = (
        P(("blk", "rel"), None),
        P(("blk", "rel")),
        P(("blk", "rel"), None),
        P(("blk", "rel")),
        P("rel", None, None),
        P(("blk", "rel"), None, None),
        P(("blk", "rel"), None, None),
        P(("blk", "rel"), None, None),
        P(("blk", "rel"), None, None),
        P(("blk", "rel"), None, None, None),
    )
    out_specs = (
        P(("blk", "rel"), None),
        P(("blk", "rel")),
        P(("blk", "rel"), None),
        P(("blk", "rel")),
        P("rel", "blk"),
    )
    return jax.shard_map(body, mesh=mesh, in_specs=in_specs, out_specs=out_specs, check_vma=False)
```

```python
import functools
import jax
import jax.numpy as jnp
from jax import lax
from jax.experimental import pallas as pl
from jax.experimental.pallas import tpu as pltpu
from jax.sharding import PartitionSpec as P

BUCKETS = 3
STEP = 0.3
NT = (((1,), (1,)), ((), ()))
TN = (((0,), (0,)), ((), ()))
VMEM_LIMIT = 60 * 1024 * 1024
MESH = pl.DeviceIdType.MESH
UNITS = 4
LANES = 512
CHUNK = 512


def onehot(index, rows):
    index = index.astype(jnp.int16)
    row = lax.broadcasted_iota(jnp.int16, (rows, index.shape[1]), 0)
    one = jnp.ones((), jnp.bfloat16)
    return jnp.where(row == index, one, jnp.zeros((), jnp.bfloat16))


def dot(a, b, dims=None):
    if dims is None:
        return jnp.dot(a, b, preferred_element_type=jnp.float32)
    return lax.dot_general(a, b, dims, preferred_element_type=jnp.float32)


def place():
    b, r = lax.axis_index("blk"), lax.axis_index("rel")
    return b // 8, (b // 4) % 2, b % 4, r // 2, r % 2


def device(z, ylo, x, yhi, core):
    return (z * 8 + ylo * 4 + x, yhi * 2 + core)


def greet(peers, swaps):
    barrier = pltpu.get_barrier_semaphore()

    def tell(peer):
        pl.semaphore_signal(barrier, inc=1, device_id=peer, device_id_type=MESH)

    for peer in peers:
        tell(peer)
    for apart, both in swaps:
        @pl.when(apart)
        def _():
            for peer in both:
                tell(peer)

    apart = sum(jnp.where(apart, 1, 0) for apart, _ in swaps)
    for n in range(len(swaps) + 1):
        @pl.when(apart == n)
        def _():
            pl.semaphore_wait(barrier, len(peers) + 2 * n)


def remote(src, dst, sems, index, peer):
    return pltpu.make_async_remote_copy(
        src_ref=src,
        dst_ref=dst,
        send_sem=sems[0].at[index],
        recv_sem=sems[1].at[index],
        device_id=peer,
        device_id_type=MESH,
    )


def send(src, dst, sems, index, peer):
    copy = remote(src, dst, sems, index, peer)
    copy.start()
    return copy


def adagrad(rows, acc, grad):
    acc = acc + jnp.sum(grad * grad, axis=0, keepdims=True) * (1.0 / grad.shape[0])
    return rows - STEP * grad * lax.rsqrt(acc), acc


def row_of(t):
    return 25 * t // 2


def last_window(s, t):
    if s == 0:
        base, top = 96 * (t // 8) + 48 * ((t // 4) % 2), 48
    elif s == 1:
        base, top = 192 * (t // 16) + 48 * ((t // 4) % 4), 48
    else:
        z = (t // 2) % 4
        base, top = 96 * (t // 8) + 16 * z + 16 * (z // 2), 32
    part = row_of(t) - base
    local = 16 * (part // 16) - 16 * (part // top)
    return base + local, local


def window(start, size):
    return pl.ds(pl.multiple_of(start, 16), size)


def total(out, own, parts):
    value = own.astype(jnp.float32)
    for part in parts:
        value = value + part.astype(jnp.float32)
    out[...] = value.astype(out.dtype)


def train_kernel(
    need_ref, slot_ref, own_ref, left_ref, lacc_ref, right_ref, racc_ref, src_ref, tgt_ref, neg_ref,
    newleft_ref, newlacc_ref, newright_ref, newracc_ref, out_ref, home_ref,
    table, fresh_ref, freshacc_ref, half, rhalf, rhalf_t, hot, query, scaled, heads_now, push, scale, score, count, sums, rows_now, acc_now,
    in_rows, in_acc, near, a0, b0, c0, a1, b1, c1, a2, b2, c2, piece, before_ref, last_ref, load_sem,
    cross_s, cross_r, ring_s, ring_r, whole_s, whole_r, pass_s, pass_r, move_s, move_r, acc_s, acc_r, near_s, near_r, sum_s, sum_r, home_s, home_r,
):
    z, ylo, x, yhi, core = place()
    me = yhi * 2 + core
    far = (1 - yhi) * 2 + core
    width, rows = newleft_ref.shape
    owned = own_ref.shape[0]
    units = owned * UNITS
    third = units // 8
    edges = src_ref.shape[2]
    nblk = slot_ref.shape[0] // BUCKETS
    block = edges // nblk
    half_rows = rows // 2
    nrel = table.shape[0]
    total_blocks = BUCKETS * nblk
    blks = 32
    b, r = lax.axis_index("blk"), lax.axis_index("rel")
    ahead, behind = ((b + 1) % blks, r), ((b + blks - 1) % blks, r)
    sibling = device(z, ylo, x, yhi, 1 - core)
    cross = device(z, 1 - ylo, x, 1 - yhi, core)
    x_ring = [device(z, ylo, (x + d) % 4, yhi, core) for d in (1, 2, 3)]
    z_ring = [device((z + d) % 4, ylo, x, yhi, core) for d in (1, 2, 3)]
    loads = [
        pltpu.make_async_copy(left_ref, newleft_ref, load_sem.at[0]),
        pltpu.make_async_copy(right_ref, rows_now, load_sem.at[1]),
    ]
    for load in loads:
        load.start()
    x_at = [(x + d) % 4 for d in (1, 2, 3)]
    z_at = [(z + d) % 4 for d in (1, 2, 3)]
    y_at = [(yhi, 1 - ylo), (1 - yhi, ylo), (1 - yhi, 1 - ylo)]
    y_ring = [device(z, v, x, h, core) for h, v in y_at]
    targets = (ylo * 16 + x * 4 + z, x * 8 + z * 2 + ylo)
    origins = ((b % 4) * 8 + (b // 16) * 4 + (b // 4) % 4, (b // 2) % 4 * 8 + (b % 2) * 4 + b // 8)
    swaps = [(to != b, ((to, r), (origin, r))) for to, origin in zip(targets, origins)]
    greet([sibling, ahead, behind] + x_ring + y_ring + z_ring, swaps)

    for j in range(owned):
        table[me * owned + j] = jnp.pad(own_ref[j], ((0, 0), (0, LANES - width)))

    def unit(owner, u):
        lanes = LANES // UNITS
        return table.at[owner * owned + u // UNITS, :, pl.ds(pl.multiple_of((u % UNITS) * lanes, lanes), lanes)]

    first = [x * third, units // 2 + z * third]
    arrivals = {}
    for i in range(third):
        for ring in range(2):
            part = unit(me, first[ring] + i)
            arrivals[ring, i] = send(part, part, (cross_s, cross_r), ring * third + i, cross)
    mine = table.at[pl.ds(me * owned, owned)]
    copies = [send(mine, mine, (whole_s, whole_r), 0, sibling)]

    def heads(t):
        for c in range(0, edges, CHUNK):
            cols = slice(c, c + CHUNK)
            hot[:, cols] = onehot(src_ref[t, :, cols], rows)
            heads_now[:, cols] = dot(half[...], hot[:, cols]).astype(jnp.bfloat16)

    def counts(t):
        found = jnp.zeros((rows, 128), jnp.float32)
        for c in range(0, edges, CHUNK):
            of = (lax.broadcasted_iota(jnp.int32, (CHUNK, 128), 0) + c) // block
            share = jnp.where(of == lax.broadcasted_iota(jnp.int32, (CHUNK, 128), 1), 1.0 / block, 0.0)
            names = [neg_ref[t, k : k + 1, :] for k in range(c // block, (c + CHUNK) // block)]
            found += dot(onehot(jnp.concatenate(names, axis=1), rows), share.astype(jnp.bfloat16))
        count[t] = found

    def chains():
        ids = [need_ref[slot_ref[n]] for n in range(total_blocks)]
        for n in range(total_blocks):
            found = jnp.int32(total_blocks)
            for m in range(n):
                found = jnp.where(ids[m] == ids[n], m, found)
            before_ref[n] = found
        for j in range(nrel):
            found = jnp.int32(total_blocks)
            for n in range(total_blocks):
                found = jnp.where(ids[n] == j, n, found)
            last_ref[j] = found

    def clear(n, carry):
        sums[n] = jnp.zeros(sums.shape[1:], sums.dtype)
        return carry

    newlacc_ref[...] = lacc_ref[...]
    acc_now[...] = racc_ref[...]
    for load in loads:
        load.wait()
    half[...] = newleft_ref[...].astype(jnp.bfloat16)
    heads(0)
    rings = (x_ring, z_ring)
    landed = {}
    for i in range(third):
        for ring in range(2):
            arrivals[ring, i].wait()
            part = unit(far, first[ring] + i)
            for d in (2, 1, 3):
                landed[ring, d, i] = send(
                    part, part, (ring_s, ring_r), (ring * 3 + d - 1) * third + i, rings[ring][d - 1]
                )
            copies.append(send(part, part, (pass_s, pass_r), ring * 4 * third + i, sibling))
        counts(i)
        if i == 1:
            chains()
            lax.fori_loop(0, sums.shape[0], clear, 0)
    for i in range(third):
        for ring in range(2):
            for d in (1, 3, 2):
                landed[ring, d, i].wait()
                origin = ((x, z)[ring] - d + 4) % 4
                part = unit(far, ring * (units // 2) + origin * third + i)
                copies.append(send(part, part, (pass_s, pass_r), (ring * 4 + d) * third + i, sibling))
    for copy in copies:
        copy.wait()

    def operator(t, k):
        return table[need_ref[slot_ref[t * nblk + k]]][:, :width]

    def earlier(n):
        return jnp.where(n < total_blocks, sums[jnp.minimum(n, total_blocks - 1)].astype(jnp.float32), 0.0)

    def moves(t, c, to_rows, to_acc):
        part = pl.ds(c * half_rows, half_rows)
        return (
            remote(fresh_ref.at[:, part], to_rows.at[:, part], (move_s, move_r), 2 * t + c, ahead),
            remote(freshacc_ref.at[:, part], to_acc.at[:, part], (acc_s, acc_r), 2 * t + c, ahead),
        )

    def queries(t):
        for k in range(nblk):
            cols = slice(k * block, (k + 1) * block)
            query[:, cols] = dot(operator(t, k), heads_now[:, cols], TN).astype(jnp.bfloat16)

    quarter = nrel // 6
    half_count = nrel // 2

    def relation(n, of_core):
        part, h, i = n // quarter, n // 2 % 2, n % 2
        return earlier(last_ref[(h * 2 + of_core) * owned + part * 2 + i])

    def staged(n):
        if n < 8:
            return push.at[pl.ds(n // 4 * width, width), pl.ds(n % 4 * LANES, LANES)]
        return in_rows.at[(n - 8) // 2, :, pl.ds(n % 2 * LANES, LANES)]

    def pair(n):
        return remote(staged(n), near.at[n], (near_s, near_r), n, sibling)

    def start(copies):
        for copy in copies:
            copy.start()

    def bucket(t, carry):
        for c in range(2):
            part = slice(c * half_rows, (c + 1) * half_rows)

            @pl.when(t > 0)
            def _():
                for move in moves(t - 1, c, in_rows.at[t - 1], in_acc.at[t - 1]):
                    move.wait()
                rows_now[:, part] = in_rows[t - 1, :, part].astype(jnp.float32)
                acc_now[:, part] = in_acc[t - 1, :, part]

            rhalf[:, part] = rows_now[:, part].astype(jnp.bfloat16)
            rhalf_t[part, :] = rhalf[:, part].T

            def meet(j):
                cols = slice(j * CHUNK, (j + 1) * CHUNK)
                value = dot(rhalf_t[part, :], query[:, cols])
                score[j % 2] = value
                target = tgt_ref[t, :, cols] - c * half_rows
                hit = lax.broadcasted_iota(jnp.int32, (half_rows, CHUNK), 0) == target
                pos = jnp.sum(jnp.where(hit, value, 0.0), axis=0, keepdims=True)
                scale[c, :, cols] = jax.nn.sigmoid(-pos)

            def weigh(j):
                cols = slice(j * CHUNK, (j + 1) * CHUNK)
                target = tgt_ref[t, :, cols] - c * half_rows
                pull = scale[c, :, cols]
                size = jnp.where((target >= 0) & (target < half_rows), jnp.maximum(pull, 2.0**-8), 1.0)
                inverse = 1.0 / size
                times = [
                    jnp.broadcast_to(count[t, part, k : k + 1], (half_rows, block)).astype(jnp.bfloat16)
                    for k in range(j * CHUNK // block, (j + 1) * CHUNK // block)
                ]
                twice = (jnp.tanh(0.5 * score[j % 2]) + 1.0).astype(jnp.bfloat16)
                push[part, cols] = twice * (0.5 * inverse).astype(jnp.bfloat16) * jnp.concatenate(
                    times, axis=1
                ) - onehot(target, half_rows) * (pull * inverse).astype(jnp.bfloat16)
                scale[c, :, cols] = size
                scaled[:, cols] = (query[:, cols].astype(jnp.float32) * size).astype(jnp.bfloat16)

            meet(0)
            for j in range(1, edges // CHUNK):
                meet(j)
                weigh(j - 1)
            weigh(edges // CHUNK - 1)
            fresh, acc = adagrad(rows_now[:, part], acc_now[:, part], dot(scaled[...], push[part, :], NT))
            fresh_ref[:, part] = fresh.astype(jnp.bfloat16)
            freshacc_ref[:, part] = acc

            @pl.when(t < BUCKETS - 1)
            def _():
                start(moves(t, c, in_rows.at[t], in_acc.at[t]))

            @pl.when(t == BUCKETS - 1)
            def _():
                start(moves(BUCKETS - 1, c, newright_ref, newracc_ref))

        for j in range(0, edges, CHUNK):
            cols = slice(j, j + CHUNK)
            scaled[:, cols] = (
                dot(rhalf[:, :half_rows], push[:half_rows, cols]) * scale[0, :, cols]
                + dot(rhalf[:, half_rows:], push[half_rows:, cols]) * scale[1, :, cols]
            ).astype(jnp.bfloat16)
        for k in range(nblk):
            cols = slice(k * block, (k + 1) * block)
            before = earlier(before_ref[t * nblk + k])
            sums[t * nblk + k] = (before + dot(heads_now[:, cols], scaled[:, cols], NT)).astype(sums.dtype)

        @pl.when(t == BUCKETS - 1)
        def _():
            for n in range(half_count):
                staged(n)[:, :width] = relation(n, 1 - core).astype(jnp.bfloat16)
                pair(n).start()

        for k in range(nblk):
            cols = slice(k * block, (k + 1) * block)
            query[:, cols] = dot(operator(t, k), scaled[:, cols]).astype(jnp.bfloat16)
        for c in range(0, rows, CHUNK):
            part = slice(c, c + CHUNK)
            left, acc = adagrad(newleft_ref[:, part], newlacc_ref[:, part], dot(query[...], hot[part, :], NT))
            newleft_ref[:, part] = left
            newlacc_ref[:, part] = acc
            half[:, part] = left.astype(jnp.bfloat16)
        @pl.when(t < BUCKETS - 1)
        def _():
            heads(t + 1)
            queries(t + 1)

        return carry

    queries(0)
    lax.fori_loop(0, BUCKETS, bucket, 0)

    sems = (sum_s, sum_r)
    own = [near.at[pl.ds(s * quarter, quarter)] for s in range(3)]
    first = []
    for s in range(3):
        for n in range(s * quarter, (s + 1) * quarter):
            pair(n).wait()
            near[n, :, :width] = (relation(n, core) + near[n, :, :width].astype(jnp.float32)).astype(jnp.bfloat16)
        for d in range(3):
            if s == 0:
                copy = send(own[s].at[:, window(96 * z_at[d], 112)], a0.at[d], sems, s * 3 + d, z_ring[d])
            elif s == 1:
                h, v = y_at[d]
                copy = send(own[s].at[pl.ds(2 * h, 2), window(192 * v, 208)], a1.at[d], sems, s * 3 + d, y_ring[d])
            else:
                copy = send(own[s].at[:, window(96 * x_at[d], 112)], a2.at[d], sems, s * 3 + d, x_ring[d])
            first.append(copy)

    second = []
    for s in range(3):
        for d in range(3):
            first[s * 3 + d].wait()
        if s == 0:
            total(a0.at[0], own[s][:, window(96 * z, 112)], [a0[d] for d in range(3)])
        elif s == 1:
            total(a1.at[0], own[s][pl.ds(2 * yhi, 2), window(192 * ylo, 208)], [a1[d] for d in range(3)])
        else:
            total(a2.at[0], own[s][:, window(96 * x, 112)], [a2[d] for d in range(3)])
        for d in range(3):
            if s == 0:
                h, v = y_at[d]
                src = a0.at[0, pl.ds(2 * h, 2), window(48 * v, 64)]
                copy = send(src, b0.at[d], sems, 9 + s * 3 + d, y_ring[d])
            elif s == 1:
                copy = send(a1.at[0, :, window(48 * x_at[d], 64)], b1.at[d], sems, 9 + s * 3 + d, x_ring[d])
            else:
                v = z_at[d]
                src = a2.at[0, :, window(16 * v + 16 * (v // 2), 48)]
                copy = send(src, b2.at[d], sems, 9 + s * 3 + d, z_ring[d])
            second.append(copy)

    def homeward(s):
        return remote(piece.at[s - 1], home_ref.at[s - 1], (home_s, home_r), s - 1, (targets[s - 1], r))

    third = []
    for s in range(3):
        for d in range(3):
            second[s * 3 + d].wait()
        if s == 0:
            total(b0.at[0], a0[0, pl.ds(2 * yhi, 2), window(48 * ylo, 64)], [b0[d] for d in range(3)])
        elif s == 1:
            total(b1.at[0], a1[0, :, window(48 * x, 64)], [b1[d] for d in range(3)])
        else:
            total(b2.at[0], a2[0, :, window(16 * z + 16 * (z // 2), 48)], [b2[d] for d in range(3)])
        for d in range(3):
            if s == 0:
                _, at = last_window(0, z * 8 + ylo * 4 + x_at[d])
                copy = send(b0.at[0, :, window(at, 32)], c0.at[d], sems, 18 + s * 3 + d, x_ring[d])
            elif s == 1:
                _, at = last_window(1, ylo * 16 + x * 4 + z_at[d])
                copy = send(b1.at[0, :, window(at, 32)], c1.at[d], sems, 18 + s * 3 + d, z_ring[d])
            else:
                h, v = y_at[d]
                _, at = last_window(2, x * 8 + z * 2 + v)
                src = b2.at[0, pl.ds(2 * h, 2), window(at, 32)]
                copy = send(src, c2.at[d], sems, 18 + s * 3 + d, y_ring[d])
            third.append(copy)

    for s in range(3):
        for d in range(3):
            third[s * 3 + d].wait()
        if s == 0:
            _, at = last_window(0, z * 8 + ylo * 4 + x)
            total(out_ref, b0[0, :, window(at, 32)], [c0[d] for d in range(3)])
        elif s == 1:
            _, at = last_window(1, ylo * 16 + x * 4 + z)
            total(piece.at[0], b1[0, :, window(at, 32)], [c1[d] for d in range(3)])
        else:
            _, at = last_window(2, x * 8 + z * 2 + ylo)
            total(piece.at[1], b2[0, pl.ds(2 * yhi, 2), window(at, 32)], [c2[d] for d in range(3)])
        if s > 0:

            @pl.when(targets[s - 1] != b)
            def _():
                homeward(s).start()

            @pl.when(targets[s - 1] == b)
            def _():
                home_ref[s - 1] = piece[s - 1]

    for s in (1, 2):

        @pl.when(targets[s - 1] != b)
        def _():
            homeward(s).wait()

    for c in range(2):
        for move in moves(BUCKETS - 1, c, newright_ref, newracc_ref):
            move.wait()


def train_call(need, slot, own, left, lacc, right, racc, src, tgt, neg, nrel, nblk):
    width, rows = left.shape
    owned = own.shape[0]
    units = owned * UNITS
    third = units // 8
    buckets, _, edges = src.shape
    dma = lambda n: [pltpu.SemaphoreType.DMA((n,))] * 2
    vmem = pl.BlockSpec(memory_space=pltpu.VMEM)
    anywhere = pl.BlockSpec(memory_space=pl.ANY)
    f32, bf16 = jnp.float32, jnp.bfloat16
    four = nrel // 6
    buf = lambda *shape: pltpu.VMEM(shape + (LANES,), bf16)
    return pl.pallas_call(
        train_kernel,
        in_specs=[pl.BlockSpec(memory_space=pltpu.SMEM)] * 2 + [vmem, anywhere, vmem, anywhere] + [vmem] * 4,
        out_specs=[vmem] * 2 + [anywhere] * 2 + [vmem] * 2,
        out_shape=[
            jax.ShapeDtypeStruct((width, rows), f32),
            jax.ShapeDtypeStruct((1, rows), f32),
            jax.ShapeDtypeStruct((width, rows), bf16),
            jax.ShapeDtypeStruct((1, rows), f32),
            jax.ShapeDtypeStruct((2, 32, LANES), f32),
            jax.ShapeDtypeStruct((2, 2, 32, LANES), bf16),
        ],
        scratch_shapes=[
            pltpu.VMEM((nrel, width, LANES), bf16),
            pltpu.VMEM((width, rows), bf16),
            pltpu.VMEM((1, rows), f32),
            pltpu.VMEM((width, rows), bf16),
            pltpu.VMEM((width, rows), bf16),
            pltpu.VMEM((rows, width), bf16),
            pltpu.VMEM((rows, edges), bf16),
            pltpu.VMEM((width, edges), bf16),
            pltpu.VMEM((width, edges), bf16),
            pltpu.VMEM((width, edges), bf16),
            pltpu.VMEM((rows, edges), bf16),
            pltpu.VMEM((2, 1, edges), f32),
            pltpu.VMEM((2, rows // 2, CHUNK), f32),
            pltpu.VMEM((buckets, rows, 128), f32),
            pltpu.VMEM((buckets * nblk, width, width), bf16),
            pltpu.VMEM((width, rows), f32),
            pltpu.VMEM((1, rows), f32),
            pltpu.VMEM((buckets - 1, width, rows), bf16),
            pltpu.VMEM((buckets - 1, 1, rows), f32),
            pltpu.VMEM((nrel // 2, width, LANES), bf16),
            buf(3, four, 112), buf(3, 2, 64), buf(3, 2, 32),
            buf(3, 2, 208), buf(3, 2, 64), buf(3, 2, 32),
            buf(3, four, 112), buf(3, four, 48), buf(3, 2, 32),
            buf(2, 2, 32),
            pltpu.SMEM((buckets * nblk,), jnp.int32),
            pltpu.SMEM((nrel,), jnp.int32),
            pltpu.SemaphoreType.DMA((2,)),
        ]
        + dma(2 * third) + dma(6 * third) + dma(1) + dma(8 * third) + dma(2 * buckets) + dma(2 * buckets) + dma(nrel // 2) + dma(27) + dma(2),
        compiler_params=pltpu.CompilerParams(
            collective_id=0, has_side_effects=True, vmem_limit_bytes=VMEM_LIMIT
        ),
        name="train_buckets",
    )(need, slot, own, left, lacc, right, racc, src, tgt, neg)


def final_share(pieces, width):
    t = lax.axis_index("blk")
    share = width * width // lax.axis_size("blk")
    rows = []
    for s in range(3):
        start, _ = last_window(s, t)
        flat = pieces[s][:, :, :width].astype(jnp.float32).reshape(2, 32 * width)
        rows.append(lax.dynamic_slice(flat, (0, t * share - start * width), (2, share)))
    return jnp.concatenate(rows, axis=0)


def body(left, left_state, right, right_state, operators, need_list, block_slot, sources, targets, negatives):
    owned_count, width, _ = operators.shape
    owners = lax.axis_size("rel")
    nrel = owned_count * owners
    src = sources[0][:, None]
    tgt = targets[0][:, None]
    neg = negatives[0]
    L, LS, R, RS, here, home = train_call(
        need_list.reshape(-1), block_slot.reshape(-1), operators, left.T, left_state[None], right.T, right_state[None], src, tgt, neg, nrel, block_slot.shape[-1]
    )
    op_grad = final_share((here, home[0], home[1]), width)
    return (L.T, LS[0], R.T.astype(jnp.float32), RS[0], op_grad)


def solution(mesh):
    in_specs = (
        P(("blk", "rel"), None),
        P(("blk", "rel")),
        P(("blk", "rel"), None),
        P(("blk", "rel")),
        P("rel", None, None),
        P(("blk", "rel"), None, None),
        P(("blk", "rel"), None, None),
        P(("blk", "rel"), None, None),
        P(("blk", "rel"), None, None),
        P(("blk", "rel"), None, None, None),
    )
    out_specs = (
        P(("blk", "rel"), None),
        P(("blk", "rel")),
        P(("blk", "rel"), None),
        P(("blk", "rel")),
        P("rel", "blk"),
    )
    return jax.shard_map(body, mesh=mesh, in_specs=in_specs, out_specs=out_specs, check_vma=False)
```

```python
import functools
import jax
import jax.numpy as jnp
from jax import lax
from jax.experimental import pallas as pl
from jax.experimental.pallas import tpu as pltpu
from jax.sharding import PartitionSpec as P

BUCKETS = 3
STEP = 0.3
NT = (((1,), (1,)), ((), ()))
TN = (((0,), (0,)), ((), ()))
VMEM_LIMIT = 60 * 1024 * 1024
MESH = pl.DeviceIdType.MESH
UNITS = 4
LANES = 512
CHUNK = 512


def onehot(index, rows):
    index = index.astype(jnp.int16)
    row = lax.broadcasted_iota(jnp.int16, (rows, index.shape[1]), 0)
    one = jnp.ones((), jnp.bfloat16)
    return jnp.where(row == index, one, jnp.zeros((), jnp.bfloat16))


def dot(a, b, dims=None):
    if dims is None:
        return jnp.dot(a, b, preferred_element_type=jnp.float32)
    return lax.dot_general(a, b, dims, preferred_element_type=jnp.float32)


def place():
    b, r = lax.axis_index("blk"), lax.axis_index("rel")
    return b // 8, (b // 4) % 2, b % 4, r // 2, r % 2


def device(z, ylo, x, yhi, core):
    return (z * 8 + ylo * 4 + x, yhi * 2 + core)


def greet(peers, swaps):
    barrier = pltpu.get_barrier_semaphore()

    def tell(peer):
        pl.semaphore_signal(barrier, inc=1, device_id=peer, device_id_type=MESH)

    for peer in peers:
        tell(peer)
    for apart, both in swaps:
        @pl.when(apart)
        def _():
            for peer in both:
                tell(peer)

    apart = sum(jnp.where(apart, 1, 0) for apart, _ in swaps)
    for n in range(len(swaps) + 1):
        @pl.when(apart == n)
        def _():
            pl.semaphore_wait(barrier, len(peers) + 2 * n)


def remote(src, dst, sems, index, peer):
    return pltpu.make_async_remote_copy(
        src_ref=src,
        dst_ref=dst,
        send_sem=sems[0].at[index],
        recv_sem=sems[1].at[index],
        device_id=peer,
        device_id_type=MESH,
    )


def send(src, dst, sems, index, peer):
    copy = remote(src, dst, sems, index, peer)
    copy.start()
    return copy


def adagrad(rows, acc, grad):
    acc = acc + jnp.sum(grad * grad, axis=0, keepdims=True) * (1.0 / grad.shape[0])
    return rows - STEP * grad * lax.rsqrt(acc), acc


def row_of(t):
    return 25 * t // 2


def last_window(s, t):
    if s == 0:
        base, top = 96 * (t // 8) + 48 * ((t // 4) % 2), 48
    elif s == 1:
        base, top = 192 * (t // 16) + 48 * ((t // 4) % 4), 48
    else:
        z = (t // 2) % 4
        base, top = 96 * (t // 8) + 16 * z + 16 * (z // 2), 32
    part = row_of(t) - base
    local = 16 * (part // 16) - 16 * (part // top)
    return base + local, local


def window(start, size):
    return pl.ds(pl.multiple_of(start, 16), size)


def total(out, own, parts):
    value = own.astype(jnp.float32)
    for part in parts:
        value = value + part.astype(jnp.float32)
    out[...] = value.astype(out.dtype)


def train_kernel(
    need_ref, slot_ref, own_ref, left_ref, lacc_ref, right_ref, racc_ref, src_ref, tgt_ref, neg_ref,
    newleft_ref, newlacc_ref, newright_ref, newracc_ref, out_ref, home_ref,
    table, fresh_ref, freshacc_ref, half, rhalf, rhalf_t, hot, query, scaled, heads_now, push, scale, score, count, sums, rows_now, acc_now,
    in_rows, in_acc, near, a0, b0, c0, a1, b1, c1, a2, b2, c2, piece, before_ref, last_ref, load_sem,
    cross_s, cross_r, ring_s, ring_r, whole_s, whole_r, pass_s, pass_r, move_s, move_r, acc_s, acc_r, near_s, near_r, sum_s, sum_r, home_s, home_r,
):
    z, ylo, x, yhi, core = place()
    me = yhi * 2 + core
    far = (1 - yhi) * 2 + core
    width, rows = newleft_ref.shape
    owned = own_ref.shape[0]
    units = owned * UNITS
    third = units // 8
    edges = src_ref.shape[2]
    nblk = slot_ref.shape[0] // BUCKETS
    block = edges // nblk
    half_rows = rows // 2
    nrel = table.shape[0]
    total_blocks = BUCKETS * nblk
    blks = 32
    b, r = lax.axis_index("blk"), lax.axis_index("rel")
    ahead, behind = ((b + 1) % blks, r), ((b + blks - 1) % blks, r)
    sibling = device(z, ylo, x, yhi, 1 - core)
    cross = device(z, 1 - ylo, x, 1 - yhi, core)
    x_ring = [device(z, ylo, (x + d) % 4, yhi, core) for d in (1, 2, 3)]
    z_ring = [device((z + d) % 4, ylo, x, yhi, core) for d in (1, 2, 3)]
    loads = [
        pltpu.make_async_copy(left_ref, newleft_ref, load_sem.at[0]),
        pltpu.make_async_copy(right_ref, rows_now, load_sem.at[1]),
    ]
    for load in loads:
        load.start()
    x_at = [(x + d) % 4 for d in (1, 2, 3)]
    z_at = [(z + d) % 4 for d in (1, 2, 3)]
    y_at = [(yhi, 1 - ylo), (1 - yhi, ylo), (1 - yhi, 1 - ylo)]
    y_ring = [device(z, v, x, h, core) for h, v in y_at]
    targets = (ylo * 16 + x * 4 + z, x * 8 + z * 2 + ylo)
    origins = ((b % 4) * 8 + (b // 16) * 4 + (b // 4) % 4, (b // 2) % 4 * 8 + (b % 2) * 4 + b // 8)
    swaps = [(to != b, ((to, r), (origin, r))) for to, origin in zip(targets, origins)]
    greet([sibling, ahead, behind] + x_ring + y_ring + z_ring, swaps)

    for j in range(owned):
        table[me * owned + j] = jnp.pad(own_ref[j], ((0, 0), (0, LANES - width)))

    def unit(owner, u):
        lanes = LANES // UNITS
        return table.at[owner * owned + u // UNITS, :, pl.ds(pl.multiple_of((u % UNITS) * lanes, lanes), lanes)]

    first = [x * third, units // 2 + z * third]
    arrivals = {}
    for i in range(third):
        for ring in range(2):
            part = unit(me, first[ring] + i)
            arrivals[ring, i] = send(part, part, (cross_s, cross_r), ring * third + i, cross)
    mine = table.at[pl.ds(me * owned, owned)]
    copies = [send(mine, mine, (whole_s, whole_r), 0, sibling)]

    def heads(t):
        for c in range(0, edges, CHUNK):
            cols = slice(c, c + CHUNK)
            hot[:, cols] = onehot(src_ref[t, :, cols], rows)
            heads_now[:, cols] = dot(half[...], hot[:, cols]).astype(jnp.bfloat16)

    def counts(t):
        found = jnp.zeros((rows, 128), jnp.float32)
        for c in range(0, edges, CHUNK):
            of = (lax.broadcasted_iota(jnp.int32, (CHUNK, 128), 0) + c) // block
            share = jnp.where(of == lax.broadcasted_iota(jnp.int32, (CHUNK, 128), 1), 1.0 / block, 0.0)
            names = [neg_ref[t, k : k + 1, :] for k in range(c // block, (c + CHUNK) // block)]
            found += dot(onehot(jnp.concatenate(names, axis=1), rows), share.astype(jnp.bfloat16))
        count[t] = found

    def chains():
        ids = [need_ref[slot_ref[n]] for n in range(total_blocks)]
        for n in range(total_blocks):
            found = jnp.int32(total_blocks)
            for m in range(n):
                found = jnp.where(ids[m] == ids[n], m, found)
            before_ref[n] = found
        for j in range(nrel):
            found = jnp.int32(total_blocks)
            for n in range(total_blocks):
                found = jnp.where(ids[n] == j, n, found)
            last_ref[j] = found

    def clear(n, carry):
        sums[n] = jnp.zeros(sums.shape[1:], sums.dtype)
        return carry

    newlacc_ref[...] = lacc_ref[...]
    acc_now[...] = racc_ref[...]
    for load in loads:
        load.wait()
    half[...] = newleft_ref[...].astype(jnp.bfloat16)
    heads(0)
    rings = (x_ring, z_ring)
    landed = {}

    def pass_arrivals(i):
        for ring in range(2):
            for d in (1, 3, 2):
                landed[ring, d, i].wait()
                origin = ((x, z)[ring] - d + 4) % 4
                part = unit(far, ring * (units // 2) + origin * third + i)
                copies.append(send(part, part, (pass_s, pass_r), (ring * 4 + d) * third + i, sibling))

    for i in range(third):
        for ring in range(2):
            arrivals[ring, i].wait()
            part = unit(far, first[ring] + i)
            for d in (2, 1, 3):
                landed[ring, d, i] = send(
                    part, part, (ring_s, ring_r), (ring * 3 + d - 1) * third + i, rings[ring][d - 1]
                )
            copies.append(send(part, part, (pass_s, pass_r), ring * 4 * third + i, sibling))
        if i > 0:
            pass_arrivals(i - 1)
        counts(i)
        if i == 1:
            chains()
            lax.fori_loop(0, sums.shape[0], clear, 0)
    pass_arrivals(third - 1)
    for copy in copies:
        copy.wait()

    def operator(t, k):
        return table[need_ref[slot_ref[t * nblk + k]]][:, :width]

    def earlier(n):
        return jnp.where(n < total_blocks, sums[jnp.minimum(n, total_blocks - 1)].astype(jnp.float32), 0.0)

    def moves(t, c, to_rows, to_acc):
        part = pl.ds(c * half_rows, half_rows)
        return (
            remote(fresh_ref.at[:, part], to_rows.at[:, part], (move_s, move_r), 2 * t + c, ahead),
            remote(freshacc_ref.at[:, part], to_acc.at[:, part], (acc_s, acc_r), 2 * t + c, ahead),
        )

    def queries(t):
        for k in range(nblk):
            cols = slice(k * block, (k + 1) * block)
            query[:, cols] = dot(operator(t, k), heads_now[:, cols], TN).astype(jnp.bfloat16)

    quarter = nrel // 6
    half_count = nrel // 2

    def relation(n, of_core):
        part, h, i = n // quarter, n // 2 % 2, n % 2
        return earlier(last_ref[(h * 2 + of_core) * owned + part * 2 + i])

    def staged(n):
        if n < 8:
            return push.at[pl.ds(n // 4 * width, width), pl.ds(n % 4 * LANES, LANES)]
        return in_rows.at[(n - 8) // 2, :, pl.ds(n % 2 * LANES, LANES)]

    def pair(n):
        return remote(staged(n), near.at[n], (near_s, near_r), n, sibling)

    def start(copies):
        for copy in copies:
            copy.start()

    def bucket(t, carry):
        for c in range(2):
            part = slice(c * half_rows, (c + 1) * half_rows)

            @pl.when(t > 0)
            def _():
                for move in moves(t - 1, c, in_rows.at[t - 1], in_acc.at[t - 1]):
                    move.wait()
                rows_now[:, part] = in_rows[t - 1, :, part].astype(jnp.float32)
                acc_now[:, part] = in_acc[t - 1, :, part]

            rhalf[:, part] = rows_now[:, part].astype(jnp.bfloat16)
            rhalf_t[part, :] = rhalf[:, part].T

            def meet(j):
                cols = slice(j * CHUNK, (j + 1) * CHUNK)
                value = dot(rhalf_t[part, :], query[:, cols])
                score[j % 2] = value
                target = tgt_ref[t, :, cols] - c * half_rows
                hit = lax.broadcasted_iota(jnp.int32, (half_rows, CHUNK), 0) == target
                pos = jnp.sum(jnp.where(hit, value, 0.0), axis=0, keepdims=True)
                scale[c, :, cols] = jax.nn.sigmoid(-pos)

            def weigh(j):
                cols = slice(j * CHUNK, (j + 1) * CHUNK)
                target = tgt_ref[t, :, cols] - c * half_rows
                pull = scale[c, :, cols]
                size = jnp.where((target >= 0) & (target < half_rows), jnp.maximum(pull, 2.0**-8), 1.0)
                inverse = 1.0 / size
                times = [
                    jnp.broadcast_to(count[t, part, k : k + 1], (half_rows, block)).astype(jnp.bfloat16)
                    for k in range(j * CHUNK // block, (j + 1) * CHUNK // block)
                ]
                twice = (jnp.tanh(0.5 * score[j % 2]) + 1.0).astype(jnp.bfloat16)
                push[part, cols] = twice * (0.5 * inverse).astype(jnp.bfloat16) * jnp.concatenate(
                    times, axis=1
                ) - onehot(target, half_rows) * (pull * inverse).astype(jnp.bfloat16)
                scale[c, :, cols] = size
                scaled[:, cols] = (query[:, cols].astype(jnp.float32) * size).astype(jnp.bfloat16)

            meet(0)
            for j in range(1, edges // CHUNK):
                meet(j)
                weigh(j - 1)
            weigh(edges // CHUNK - 1)
            fresh, acc = adagrad(rows_now[:, part], acc_now[:, part], dot(scaled[...], push[part, :], NT))
            fresh_ref[:, part] = fresh.astype(jnp.bfloat16)
            freshacc_ref[:, part] = acc

            @pl.when(t < BUCKETS - 1)
            def _():
                start(moves(t, c, in_rows.at[t], in_acc.at[t]))

            @pl.when(t == BUCKETS - 1)
            def _():
                start(moves(BUCKETS - 1, c, newright_ref, newracc_ref))

        for j in range(0, edges, CHUNK):
            cols = slice(j, j + CHUNK)
            scaled[:, cols] = (
                dot(rhalf[:, :half_rows], push[:half_rows, cols]) * scale[0, :, cols]
                + dot(rhalf[:, half_rows:], push[half_rows:, cols]) * scale[1, :, cols]
            ).astype(jnp.bfloat16)
        for k in range(nblk):
            cols = slice(k * block, (k + 1) * block)
            before = earlier(before_ref[t * nblk + k])
            sums[t * nblk + k] = (before + dot(heads_now[:, cols], scaled[:, cols], NT)).astype(sums.dtype)

        @pl.when(t == BUCKETS - 1)
        def _():
            for n in [(m + quarter) % half_count for m in range(half_count)]:
                staged(n)[:, :width] = relation(n, 1 - core).astype(jnp.bfloat16)
                pair(n).start()

        for k in range(nblk):
            cols = slice(k * block, (k + 1) * block)
            query[:, cols] = dot(operator(t, k), scaled[:, cols]).astype(jnp.bfloat16)
        for c in range(0, rows, CHUNK):
            part = slice(c, c + CHUNK)
            left, acc = adagrad(newleft_ref[:, part], newlacc_ref[:, part], dot(query[...], hot[part, :], NT))
            newleft_ref[:, part] = left
            newlacc_ref[:, part] = acc
            half[:, part] = left.astype(jnp.bfloat16)
        @pl.when(t < BUCKETS - 1)
        def _():
            heads(t + 1)
            queries(t + 1)

        return carry

    queries(0)
    lax.fori_loop(0, BUCKETS, bucket, 0)

    sems = (sum_s, sum_r)
    own = [near.at[pl.ds(s * quarter, quarter)] for s in range(3)]
    first = {}
    for s in (1, 2, 0):
        for n in range(s * quarter, (s + 1) * quarter):
            pair(n).wait()
            near[n, :, :width] = (relation(n, core) + near[n, :, :width].astype(jnp.float32)).astype(jnp.bfloat16)
        for d in range(3):
            if s == 0:
                copy = send(own[s].at[:, window(96 * z_at[d], 112)], a0.at[d], sems, s * 3 + d, z_ring[d])
            elif s == 1:
                h, v = y_at[d]
                copy = send(own[s].at[pl.ds(2 * h, 2), window(192 * v, 208)], a1.at[d], sems, s * 3 + d, y_ring[d])
            else:
                copy = send(own[s].at[:, window(96 * x_at[d], 112)], a2.at[d], sems, s * 3 + d, x_ring[d])
            first[s, d] = copy

    second = {}
    for s in (1, 2, 0):
        for d in range(3):
            first[s, d].wait()
        if s == 0:
            total(a0.at[0], own[s][:, window(96 * z, 112)], [a0[d] for d in range(3)])
        elif s == 1:
            total(a1.at[0], own[s][pl.ds(2 * yhi, 2), window(192 * ylo, 208)], [a1[d] for d in range(3)])
        else:
            total(a2.at[0], own[s][:, window(96 * x, 112)], [a2[d] for d in range(3)])
        for d in range(3):
            if s == 0:
                h, v = y_at[d]
                src = a0.at[0, pl.ds(2 * h, 2), window(48 * v, 64)]
                copy = send(src, b0.at[d], sems, 9 + s * 3 + d, y_ring[d])
            elif s == 1:
                copy = send(a1.at[0, :, window(48 * x_at[d], 64)], b1.at[d], sems, 9 + s * 3 + d, x_ring[d])
            else:
                v = z_at[d]
                src = a2.at[0, :, window(16 * v + 16 * (v // 2), 48)]
                copy = send(src, b2.at[d], sems, 9 + s * 3 + d, z_ring[d])
            second[s, d] = copy

    def homeward(s):
        return remote(piece.at[s - 1], home_ref.at[s - 1], (home_s, home_r), s - 1, (targets[s - 1], r))

    third = {}
    for s in (1, 2, 0):
        for d in range(3):
            second[s, d].wait()
        if s == 0:
            total(b0.at[0], a0[0, pl.ds(2 * yhi, 2), window(48 * ylo, 64)], [b0[d] for d in range(3)])
        elif s == 1:
            total(b1.at[0], a1[0, :, window(48 * x, 64)], [b1[d] for d in range(3)])
        else:
            total(b2.at[0], a2[0, :, window(16 * z + 16 * (z // 2), 48)], [b2[d] for d in range(3)])
        for d in range(3):
            if s == 0:
                _, at = last_window(0, z * 8 + ylo * 4 + x_at[d])
                copy = send(b0.at[0, :, window(at, 32)], c0.at[d], sems, 18 + s * 3 + d, x_ring[d])
            elif s == 1:
                _, at = last_window(1, ylo * 16 + x * 4 + z_at[d])
                copy = send(b1.at[0, :, window(at, 32)], c1.at[d], sems, 18 + s * 3 + d, z_ring[d])
            else:
                h, v = y_at[d]
                _, at = last_window(2, x * 8 + z * 2 + v)
                src = b2.at[0, pl.ds(2 * h, 2), window(at, 32)]
                copy = send(src, c2.at[d], sems, 18 + s * 3 + d, y_ring[d])
            third[s, d] = copy

    for s in (1, 2, 0):
        for d in range(3):
            third[s, d].wait()
        if s == 0:
            _, at = last_window(0, z * 8 + ylo * 4 + x)
            total(out_ref, b0[0, :, window(at, 32)], [c0[d] for d in range(3)])
        elif s == 1:
            _, at = last_window(1, ylo * 16 + x * 4 + z)
            total(piece.at[0], b1[0, :, window(at, 32)], [c1[d] for d in range(3)])
        else:
            _, at = last_window(2, x * 8 + z * 2 + ylo)
            total(piece.at[1], b2[0, pl.ds(2 * yhi, 2), window(at, 32)], [c2[d] for d in range(3)])
        if s > 0:

            @pl.when(targets[s - 1] != b)
            def _():
                homeward(s).start()

            @pl.when(targets[s - 1] == b)
            def _():
                home_ref[s - 1] = piece[s - 1]

    for s in (1, 2):

        @pl.when(targets[s - 1] != b)
        def _():
            homeward(s).wait()

    for c in range(2):
        for move in moves(BUCKETS - 1, c, newright_ref, newracc_ref):
            move.wait()


def train_call(need, slot, own, left, lacc, right, racc, src, tgt, neg, nrel, nblk):
    width, rows = left.shape
    owned = own.shape[0]
    units = owned * UNITS
    third = units // 8
    buckets, _, edges = src.shape
    dma = lambda n: [pltpu.SemaphoreType.DMA((n,))] * 2
    vmem = pl.BlockSpec(memory_space=pltpu.VMEM)
    anywhere = pl.BlockSpec(memory_space=pl.ANY)
    f32, bf16 = jnp.float32, jnp.bfloat16
    four = nrel // 6
    buf = lambda *shape: pltpu.VMEM(shape + (LANES,), bf16)
    return pl.pallas_call(
        train_kernel,
        in_specs=[pl.BlockSpec(memory_space=pltpu.SMEM)] * 2 + [vmem, anywhere, vmem, anywhere] + [vmem] * 4,
        out_specs=[vmem] * 2 + [anywhere] * 2 + [vmem] * 2,
        out_shape=[
            jax.ShapeDtypeStruct((width, rows), f32),
            jax.ShapeDtypeStruct((1, rows), f32),
            jax.ShapeDtypeStruct((width, rows), bf16),
            jax.ShapeDtypeStruct((1, rows), f32),
            jax.ShapeDtypeStruct((2, 32, LANES), f32),
            jax.ShapeDtypeStruct((2, 2, 32, LANES), bf16),
        ],
        scratch_shapes=[
            pltpu.VMEM((nrel, width, LANES), bf16),
            pltpu.VMEM((width, rows), bf16),
            pltpu.VMEM((1, rows), f32),
            pltpu.VMEM((width, rows), bf16),
            pltpu.VMEM((width, rows), bf16),
            pltpu.VMEM((rows, width), bf16),
            pltpu.VMEM((rows, edges), bf16),
            pltpu.VMEM((width, edges), bf16),
            pltpu.VMEM((width, edges), bf16),
            pltpu.VMEM((width, edges), bf16),
            pltpu.VMEM((rows, edges), bf16),
            pltpu.VMEM((2, 1, edges), f32),
            pltpu.VMEM((2, rows // 2, CHUNK), f32),
            pltpu.VMEM((buckets, rows, 128), f32),
            pltpu.VMEM((buckets * nblk, width, width), bf16),
            pltpu.VMEM((width, rows), f32),
            pltpu.VMEM((1, rows), f32),
            pltpu.VMEM((buckets - 1, width, rows), bf16),
            pltpu.VMEM((buckets - 1, 1, rows), f32),
            pltpu.VMEM((nrel // 2, width, LANES), bf16),
            buf(3, four, 112), buf(3, 2, 64), buf(3, 2, 32),
            buf(3, 2, 208), buf(3, 2, 64), buf(3, 2, 32),
            buf(3, four, 112), buf(3, four, 48), buf(3, 2, 32),
            buf(2, 2, 32),
            pltpu.SMEM((buckets * nblk,), jnp.int32),
            pltpu.SMEM((nrel,), jnp.int32),
            pltpu.SemaphoreType.DMA((2,)),
        ]
        + dma(2 * third) + dma(6 * third) + dma(1) + dma(8 * third) + dma(2 * buckets) + dma(2 * buckets) + dma(nrel // 2) + dma(27) + dma(2),
        compiler_params=pltpu.CompilerParams(
            collective_id=0, has_side_effects=True, vmem_limit_bytes=VMEM_LIMIT
        ),
        name="train_buckets",
    )(need, slot, own, left, lacc, right, racc, src, tgt, neg)


def final_share(pieces, width):
    t = lax.axis_index("blk")
    share = width * width // lax.axis_size("blk")
    rows = []
    for s in range(3):
        start, _ = last_window(s, t)
        flat = pieces[s][:, :, :width].astype(jnp.float32).reshape(2, 32 * width)
        rows.append(lax.dynamic_slice(flat, (0, t * share - start * width), (2, share)))
    return jnp.concatenate(rows, axis=0)


def body(left, left_state, right, right_state, operators, need_list, block_slot, sources, targets, negatives):
    owned_count, width, _ = operators.shape
    owners = lax.axis_size("rel")
    nrel = owned_count * owners
    src = sources[0][:, None]
    tgt = targets[0][:, None]
    neg = negatives[0]
    L, LS, R, RS, here, home = train_call(
        need_list.reshape(-1), block_slot.reshape(-1), operators, left.T, left_state[None], right.T, right_state[None], src, tgt, neg, nrel, block_slot.shape[-1]
    )
    op_grad = final_share((here, home[0], home[1]), width)
    return (L.T, LS[0], R.T.astype(jnp.float32), RS[0], op_grad)


def solution(mesh):
    in_specs = (
        P(("blk", "rel"), None),
        P(("blk", "rel")),
        P(("blk", "rel"), None),
        P(("blk", "rel")),
        P("rel", None, None),
        P(("blk", "rel"), None, None),
        P(("blk", "rel"), None, None),
        P(("blk", "rel"), None, None),
        P(("blk", "rel"), None, None),
        P(("blk", "rel"), None, None, None),
    )
    out_specs = (
        P(("blk", "rel"), None),
        P(("blk", "rel")),
        P(("blk", "rel"), None),
        P(("blk", "rel")),
        P("rel", "blk"),
    )
    return jax.shard_map(body, mesh=mesh, in_specs=in_specs, out_specs=out_specs, check_vma=False)
```
